512 devices in a mesh: tm: 8 (over y_lo, x), chan: 64 (over z, y_hi, core).
Axes of the slice: x: 4, y: 8 (y_hi: 4, y_lo: 2; y = y_hi * 2 + y_lo), z: 8, core: 2. Of those that a mesh axis runs over, the one named last changes fastest.
Arguments:
- voltages: int32 [256, 1048576], P('chan', 'tm'), may hold values from 0 to 4095
- beam_weights: int32 [64, 768, 256], P('chan'), may hold values from 0 to 4095
Outputs:
- beam_powers: float32 [8, 768, 8192], P('tm', 'chan')
The draws below stay inside these ranges and needn't reach their ends.
All inputs are finite; a program needn't handle non-finite values.
Results may differ from the reference program's by a relative error of at most 0.00098.
Values may be sent and summed in bfloat16 or wider, within the bound.
No kernel may reach another device: no remote copies, remote signals or barrier semaphores. Data moves between devices by JAX's collectives and lax.ppermute only.
A program may use at most 128 MiB of HBM per device.

```python
import math
import jax
import jax.numpy as jnp
from jax import lax

INPUTS = 256
BEAMS = 768
CHANNELS = 8192
TAPS = 4
AVERAGE = 16
WEIGHT_BLOCK = 128
SPECTRA_DEV = 16
WEIGHT_GROUPS = 64
SAMPLES = 1048576
N_TM = 8


def with_ends(values, key, smallest, top_value):
    longest = values.shape.index(max(values.shape))
    spots = []
    for shift in (0, 1):
        where = [jax.random.randint(jax.random.fold_in(key, axis), (), 0, length) for axis, length in enumerate(values.shape)]
        where[longest] = (where[longest] + shift) % values.shape[longest]
        spots.append(tuple(where))
    return values.at[spots[0]].set(smallest).at[spots[1]].set(top_value)


def setup_inputs(seed: int = 0) -> dict:
    keys = jax.random.split(jax.random.key(seed), 3)
    voltages = with_ends(jax.random.randint(keys[0], (INPUTS, SAMPLES), 0, 4096), jax.random.fold_in(keys[0], 1), 0, 4095).astype(jnp.int32)
    beam_weights = with_ends(jax.random.randint(keys[1], (WEIGHT_GROUPS, BEAMS, INPUTS), 0, 4096), jax.random.fold_in(keys[1], 1), 0, 4095).astype(jnp.int32)
    return {"voltages": voltages, "beam_weights": beam_weights}


def unpack_pair(packed):
    real_part = (packed // 64 - 32).astype(jnp.float32)
    imag_part = (packed % 64 - 32).astype(jnp.float32)
    return (real_part, imag_part)

def pfb_taper():
    length = TAPS * CHANNELS
    places = jnp.arange(length, dtype=jnp.int32).astype(jnp.float32)
    offsets = (places - 0.5 * length + 0.5) / CHANNELS
    hann_window = 0.5 - 0.5 * jnp.cos(2.0 * math.pi * (places + 0.5) / length)
    return (jnp.sinc(offsets) * hann_window).reshape(TAPS, CHANNELS)

def stacked_weights(packed):
    real_part, imag_part = unpack_pair(packed)
    upper_rows = jnp.concatenate([real_part, -imag_part], axis=-1)
    lower_rows = jnp.concatenate([imag_part, real_part], axis=-1)
    return jnp.concatenate([upper_rows, lower_rows], axis=-2).astype(jnp.bfloat16)

def reference(voltages, beam_weights):
    inputs_all = voltages.shape[0]
    group_len = SPECTRA_DEV * CHANNELS
    rim_len = (TAPS - 1) * CHANNELS
    grouped = jnp.transpose(voltages.reshape(inputs_all, N_TM, group_len), (1, 0, 2))
    previous = jnp.concatenate([grouped[:1, :, :rim_len], grouped[:-1, :, group_len - rim_len:]], axis=0)
    present = (jnp.arange(N_TM, dtype=jnp.int32) > 0).astype(jnp.float32)
    coeffs = pfb_taper()
    dft_norm = 1.0 / (32.0 * math.sqrt(CHANNELS))
    beam_scale = 1.0 / (24.0 * math.sqrt(INPUTS))
    block_count = CHANNELS // WEIGHT_BLOCK
    mean_count = SPECTRA_DEV // AVERAGE

    def one_group(packed_group):
        own_packed, before, present_flag = packed_group
        own_real, own_imag = unpack_pair(own_packed)
        old_real, old_imag = unpack_pair(before)
        stream_real = jnp.concatenate([old_real * present_flag, own_real], axis=1)
        stream_imag = jnp.concatenate([old_imag * present_flag, own_imag], axis=1)

        def tap_sum(stream):
            summed = jnp.zeros((inputs_all, SPECTRA_DEV, CHANNELS), jnp.float32)
            for tap_index in range(TAPS):
                window_piece = lax.slice_in_dim(stream, tap_index * CHANNELS, (tap_index + SPECTRA_DEV) * CHANNELS, axis=1)
                summed = summed + window_piece.reshape(inputs_all, SPECTRA_DEV, CHANNELS) * coeffs[tap_index]
            return summed
        spectra = jnp.fft.fft(tap_sum(stream_real) + 1j * tap_sum(stream_imag), axis=-1) * dft_norm
        pieces = jnp.stack([spectra.real, spectra.imag]).astype(jnp.bfloat16)
        pieces = pieces.reshape(2 * inputs_all, SPECTRA_DEV, block_count, WEIGHT_BLOCK)
        pieces = jnp.transpose(pieces, (2, 0, 1, 3))

        def one_block(paired):
            channel_block, packed_block = paired
            formed = jnp.dot(stacked_weights(packed_block), channel_block.reshape(2 * inputs_all, SPECTRA_DEV * WEIGHT_BLOCK), preferred_element_type=jnp.float32)
            beam_real = formed[:BEAMS] * beam_scale
            beam_imag = formed[BEAMS:] * beam_scale
            powers = (beam_real * beam_real + beam_imag * beam_imag).reshape(BEAMS, mean_count, AVERAGE, WEIGHT_BLOCK)
            return lax.optimization_barrier(jnp.mean(powers, axis=2))
        averaged = lax.map(one_block, (pieces, beam_weights))
        return jnp.transpose(averaged, (2, 1, 0, 3)).reshape(mean_count, BEAMS, CHANNELS)
    result = lax.map(one_group, (grouped, previous, present))
    return result.reshape(N_TM * mean_count, BEAMS, CHANNELS)
```

```python
import functools
import math

import jax
import jax.numpy as jnp
import numpy as np
from jax import lax
from jax.experimental import pallas as pl
from jax.experimental.pallas import tpu as pltpu
from jax.sharding import PartitionSpec as P

INPUTS = 256
BEAMS = 768
CHANNELS = 8192
SECTION = 128
TAPS = 4
AVERAGE = 16
OUTER = 64
GROUPS = 64
ZERO_SAMPLE = 32 * 64 + 32
VMEM_BYTES = 48 * 1024 * 1024

INPUTS_HERE = 4
FRAME_ROWS = OUTER * INPUTS_HERE
PAIR_ROWS = 16


def split_table(table):
    high = table.astype(jnp.bfloat16)
    low = (table - np.asarray(high, np.float64)).astype(jnp.bfloat16)
    return np.asarray(high), np.asarray(low)


def pfb_taper():
    places = np.arange(TAPS * CHANNELS, dtype=np.float64)
    length = TAPS * CHANNELS
    offsets = (places - 0.5 * length + 0.5) / CHANNELS
    hann_window = 0.5 - 0.5 * np.cos(2.0 * math.pi * (places + 0.5) / length)
    taper = np.sinc(offsets) * hann_window
    return taper.astype(np.float32).reshape(TAPS, OUTER, SECTION)


def phasors(left_index, right_index, length):
    turns = np.outer(left_index, right_index) % length
    angles = turns * (-2.0 * math.pi / length)
    return np.cos(angles), np.sin(angles)


def outer_table():
    cos_part, sin_part = phasors(np.arange(OUTER), np.arange(OUTER), OUTER)
    table = np.zeros((2, 2, OUTER, 2, 2, OUTER))
    for f in range(2):
        table[0, f, :, f, 0, :] = cos_part
        table[0, f, :, f, 1, :] = -sin_part
        table[1, f, :, f, 0, :] = sin_part
        table[1, f, :, f, 1, :] = cos_part
    return table.reshape(4 * OUTER, 4 * OUTER)


def twist_table():
    norm = 1.0 / (32.0 * math.sqrt(CHANNELS))
    cos_part, sin_part = phasors(np.arange(OUTER), np.arange(SECTION), CHANNELS)
    return (
        np.tile(cos_part * norm, (2, 1)).astype(np.float32),
        np.tile(sin_part * norm, (2, 1)).astype(np.float32),
    )


def inner_table():
    channel = np.arange(SECTION).reshape(GROUPS, 2).T
    table = np.zeros((2, 2, GROUPS, 2, SECTION))
    for half in range(2):
        cos_part, sin_part = phasors(channel[half], np.arange(SECTION), SECTION)
        table[half, 0, :, 0, :] = cos_part
        table[half, 0, :, 1, :] = -sin_part
        table[half, 1, :, 0, :] = sin_part
        table[half, 1, :, 1, :] = cos_part
    return table.reshape(4 * GROUPS, 2 * SECTION)


def two_halves(values):
    high = values.astype(jnp.bfloat16)
    low = (values - high.astype(jnp.float32)).astype(jnp.bfloat16)
    return high, low


def careful_dot(left_high, left_low, right, contract):
    right_high, right_low = two_halves(right)
    dims = (contract, ((), ()))

    def dot(left, values):
        return lax.dot_general(left, values, dims, preferred_element_type=jnp.float32)

    return dot(left_high, right_high) + (dot(left_high, right_low) + dot(left_low, right_high))


def channelize_kernel(
    frame0, frame1, frame2, frame3, frame4, taper,
    outer_high, outer_low, twist_cos, twist_sin, inner_high, inner_low,
    out, strided,
):
    packed_frames = (frame0, frame1, frame2, frame3, frame4)
    columns = []
    for i in range(INPUTS_HERE):
        summed = {}
        for t, packed_ref in enumerate(packed_frames):
            packed = packed_ref[pl.ds(i, OUTER, stride=INPUTS_HERE), :]
            parts = (
                ((packed >> 6) - 32).astype(jnp.float32),
                ((packed & 63) - 32).astype(jnp.float32),
            )
            for f in range(2):
                if 0 <= t - f < TAPS:
                    for part in range(2):
                        term = parts[part] * taper[t - f]
                        key = (f, part)
                        summed[key] = summed[key] + term if key in summed else term
        columns.append(
            jnp.concatenate([summed[f, part] for f in range(2) for part in range(2)], axis=0)
        )
    frames = jnp.concatenate(columns, axis=1)
    first = careful_dot(outer_high[...], outer_low[...], frames, ((1,), (0,)))
    cos_part, sin_part = twist_cos[...], twist_sin[...]
    turned = []
    for i in range(INPUTS_HERE):
        real_part = first[:SECTION, i * SECTION : (i + 1) * SECTION]
        imag_part = first[SECTION:, i * SECTION : (i + 1) * SECTION]
        turned.append(
            jnp.concatenate(
                [
                    real_part * cos_part - imag_part * sin_part,
                    real_part * sin_part + imag_part * cos_part,
                ],
                axis=1,
            )
        )
    turned = jnp.concatenate(turned, axis=0)
    spectra = careful_dot(inner_high[...], inner_low[...], turned, ((1,), (1,)))
    for half in range(2):
        for part in range(2):
            top = (half * 2 + part) * GROUPS
            for i in range(INPUTS_HERE):
                row = half * 8 + i * 2 + part
                strided[pl.ds(row, GROUPS, stride=PAIR_ROWS), :] = spectra[
                    top : top + GROUPS, i * SECTION : (i + 1) * SECTION
                ]
    out[...] = strided[...].astype(jnp.bfloat16).reshape(out.shape)


def channelize(packed_rows, first_frame, pairs):
    outer_high, outer_low = split_table(outer_table())
    inner_high, inner_low = split_table(inner_table())
    twist_cos, twist_sin = twist_table()
    tables = (pfb_taper(), outer_high, outer_low, twist_cos, twist_sin, inner_high, inner_low)

    def frame_spec(t):
        return pl.BlockSpec((FRAME_ROWS, SECTION), lambda pair: (first_frame + 2 * pair + t, 0))

    def whole(table):
        return pl.BlockSpec(table.shape, lambda pair: (0,) * table.ndim)

    return pl.pallas_call(
        channelize_kernel,
        grid=(pairs,),
        in_specs=[frame_spec(t) for t in range(5)] + [whole(table) for table in tables],
        out_specs=pl.BlockSpec((GROUPS, 1, PAIR_ROWS, SECTION), lambda pair: (0, pair, 0, 0)),
        out_shape=jax.ShapeDtypeStruct((GROUPS, pairs, PAIR_ROWS, SECTION), jnp.bfloat16),
        scratch_shapes=[pltpu.VMEM((GROUPS * PAIR_ROWS, SECTION), jnp.float32)],
        compiler_params=pltpu.CompilerParams(vmem_limit_bytes=VMEM_BYTES),
        cost_estimate=pl.CostEstimate(
            flops=pairs * 3 * 2 * 2 * 256 * 256 * 512,
            bytes_accessed=pairs * (5 * 131072 + 262144),
            transcendentals=0,
        ),
        name="channelize",
    )(*([packed_rows] * 5), *(jnp.asarray(table) for table in tables))


def spread_tables():
    even = np.zeros((INPUTS, INPUTS, 2))
    odd = np.zeros((INPUTS, INPUTS, 2))
    even[np.arange(INPUTS), np.arange(INPUTS), 0] = 1.0
    odd[np.arange(INPUTS), np.arange(INPUTS), 1] = 1.0
    even = even.reshape(INPUTS, 2 * INPUTS)
    odd = odd.reshape(INPUTS, 2 * INPUTS)
    upper = np.concatenate([even, -odd], axis=0)
    lower = np.concatenate([odd, even], axis=0)
    return upper.astype(jnp.bfloat16), lower.astype(jnp.bfloat16)


def weights_kernel(packed_ref, upper, lower, out):
    packed = packed_ref[...]
    parts = jnp.concatenate(
        [
            ((packed >> 6) - 32).astype(jnp.float32).astype(jnp.bfloat16),
            ((packed & 63) - 32).astype(jnp.float32).astype(jnp.bfloat16),
        ],
        axis=1,
    )
    out[:BEAMS] = jnp.dot(parts, upper[...], preferred_element_type=jnp.float32).astype(
        jnp.bfloat16
    )
    out[BEAMS:] = jnp.dot(parts, lower[...], preferred_element_type=jnp.float32).astype(
        jnp.bfloat16
    )


def stacked_weights(packed):
    upper, lower = spread_tables()
    return pl.pallas_call(
        weights_kernel,
        out_shape=jax.ShapeDtypeStruct((2 * BEAMS, 2 * INPUTS), jnp.bfloat16),
        in_specs=[pl.BlockSpec(memory_space=pltpu.VMEM)] * 3,
        out_specs=pl.BlockSpec(memory_space=pltpu.VMEM),
        compiler_params=pltpu.CompilerParams(vmem_limit_bytes=VMEM_BYTES),
        cost_estimate=pl.CostEstimate(
            flops=2 * 2 * BEAMS * 512 * 512, bytes_accessed=5 * 2**20, transcendentals=0
        ),
        name="stack_weights",
    )(packed, jnp.asarray(upper), jnp.asarray(lower))


def beam_block(weights_ref, spectra_ref):
    spectra = spectra_ref[...].astype(jnp.float32).reshape(GROUPS, PAIR_ROWS, SECTION)
    paired = jnp.concatenate(
        [
            spectra[:, half * 8 : half * 8 + 8].reshape(2 * INPUTS, SECTION).astype(jnp.bfloat16)
            for half in range(2)
        ],
        axis=1,
    )
    formed = jnp.dot(weights_ref[...], paired, preferred_element_type=jnp.float32)
    real_part, imag_part = formed[:BEAMS], formed[BEAMS:]
    return real_part * real_part + imag_part * imag_part


def start_kernel(weights_ref, spectra_ref, out):
    powers = beam_block(weights_ref, spectra_ref)

    @pl.when(pl.program_id(0) == 0)
    def _():
        out[...] = powers

    @pl.when(pl.program_id(0) > 0)
    def _():
        out[...] += powers


def finish_kernel(weights_ref, spectra_ref, before, out, total):
    powers = beam_block(weights_ref, spectra_ref)

    @pl.when(pl.program_id(0) == 0)
    def _():
        total[...] = before[...] + powers

    @pl.when(pl.program_id(0) > 0)
    def _():
        total[...] += powers

    @pl.when(pl.program_id(0) == pl.num_programs(0) - 1)
    def _():
        scale = 1.0 / (24.0 * math.sqrt(INPUTS)) ** 2 / AVERAGE
        sums = []
        for half in range(2):
            part = total[:, half * SECTION : (half + 1) * SECTION]
            sums.append((part + pltpu.roll(part, OUTER, 1)) * scale)
        lane = lax.broadcasted_iota(jnp.int32, (BEAMS, SECTION), 1)
        out[...] = jnp.where(lane < OUTER, sums[0], sums[1])


def beam_call(weights, spectra, before=None):
    pairs = spectra.shape[1]
    in_specs = [
        pl.BlockSpec((2 * BEAMS, 2 * INPUTS), lambda pair: (0, 0)),
        pl.BlockSpec((GROUPS, 1, PAIR_ROWS, SECTION), lambda pair: (0, pair, 0, 0)),
    ]
    operands = [weights, spectra]
    width = 2 * SECTION
    scratch = []
    if before is not None:
        in_specs.append(pl.BlockSpec((BEAMS, width), lambda pair: (0, 0)))
        operands.append(before)
        scratch.append(pltpu.VMEM((BEAMS, width), jnp.float32))
        width = SECTION
    return pl.pallas_call(
        start_kernel if before is None else finish_kernel,
        grid=(pairs,),
        in_specs=in_specs,
        out_specs=pl.BlockSpec((BEAMS, width), lambda pair: (0, 0)),
        out_shape=jax.ShapeDtypeStruct((BEAMS, width), jnp.float32),
        scratch_shapes=scratch,
        compiler_params=pltpu.CompilerParams(vmem_limit_bytes=VMEM_BYTES),
        cost_estimate=pl.CostEstimate(
            flops=pairs * 2 * 1536 * 512 * 256,
            bytes_accessed=1536 * 512 * 2 + pairs * 262144 + 3 * 768 * 256 * 4,
            transcendentals=0,
        ),
        name="beams_start" if before is None else "beams_finish",
    )(*operands)


LATE_PAIRS = 4


def per_device(voltages, beam_weights):
    inputs_here, own_len = voltages.shape
    spectra_here = own_len // CHANNELS
    rows = jnp.transpose(voltages.reshape(inputs_here, own_len // SECTION, SECTION), (1, 0, 2))
    rows = rows.reshape(own_len // SECTION * inputs_here, SECTION)
    rim = (TAPS - 1) * FRAME_ROWS
    devices = lax.axis_size("tm")
    history = lax.ppermute(
        rows[rows.shape[0] - rim :] - ZERO_SAMPLE,
        "tm",
        [(i, i + 1) for i in range(devices - 1)],
    )
    late = 2 * LATE_PAIRS
    late_spectra = channelize(rows, spectra_here - late - 3, LATE_PAIRS)
    late_turned = lax.all_to_all(late_spectra, "chan", 0, 0, tiled=True)
    early = spectra_here - late
    early_rows = jnp.concatenate([history + ZERO_SAMPLE, rows[: early * FRAME_ROWS]], axis=0)
    early_spectra = channelize(early_rows, 0, early // 2)
    early_turned = lax.all_to_all(early_spectra, "chan", 0, 0, tiled=True)
    weights = stacked_weights(beam_weights[0])
    powers = beam_call(weights, late_turned)
    averaged = beam_call(weights, early_turned, powers)
    return lax.all_to_all(averaged[None], "chan", split_axis=1, concat_axis=2, tiled=True)


def solution(mesh):
    return jax.shard_map(
        per_device,
        mesh=mesh,
        in_specs=(P("chan", "tm"), P("chan", None, None)),
        out_specs=P("tm", "chan", None),
        check_vma=False,
    )
```

```python
import functools
import math

import jax
import jax.numpy as jnp
import numpy as np
from jax import lax
from jax.experimental import pallas as pl
from jax.experimental.pallas import tpu as pltpu
from jax.sharding import PartitionSpec as P

INPUTS = 256
BEAMS = 768
CHANNELS = 8192
SECTION = 128
TAPS = 4
AVERAGE = 16
OUTER = 64
GROUPS = 64
ZERO_SAMPLE = 32 * 64 + 32
VMEM_BYTES = 60 * 1024 * 1024
BEAM_VMEM_BYTES = 32 * 1024 * 1024

INPUTS_HERE = 4
FRAME_ROWS = OUTER * INPUTS_HERE
PAIR_ROWS = 16


def split_table(table):
    high = table.astype(jnp.bfloat16)
    low = (table - np.asarray(high, np.float64)).astype(jnp.bfloat16)
    return np.asarray(high), np.asarray(low)


def pfb_taper():
    places = np.arange(TAPS * CHANNELS, dtype=np.float64)
    length = TAPS * CHANNELS
    offsets = (places - 0.5 * length + 0.5) / CHANNELS
    hann_window = 0.5 - 0.5 * np.cos(2.0 * math.pi * (places + 0.5) / length)
    taper = np.sinc(offsets) * hann_window
    return taper.astype(np.float32).reshape(TAPS, OUTER, SECTION)


def phasors(left_index, right_index, length):
    turns = np.outer(left_index, right_index) % length
    angles = turns * (-2.0 * math.pi / length)
    return np.cos(angles), np.sin(angles)


def outer_table():
    cos_part, sin_part = phasors(np.arange(OUTER), np.arange(OUTER), OUTER)
    table = np.zeros((2, 2, OUTER, 2, 2, OUTER))
    for f in range(2):
        table[0, f, :, f, 0, :] = cos_part
        table[0, f, :, f, 1, :] = -sin_part
        table[1, f, :, f, 0, :] = sin_part
        table[1, f, :, f, 1, :] = cos_part
    return table.reshape(4 * OUTER, 4 * OUTER)


def twist_table():
    norm = 1.0 / (32.0 * math.sqrt(CHANNELS))
    cos_part, sin_part = phasors(np.arange(OUTER), np.arange(SECTION), CHANNELS)
    return (
        np.tile(cos_part * norm, (2, 1)).astype(np.float32),
        np.tile(sin_part * norm, (2, 1)).astype(np.float32),
    )


def inner_table():
    channel = np.arange(SECTION).reshape(GROUPS, 2).T
    table = np.zeros((2, 2, GROUPS, 2, SECTION))
    for half in range(2):
        cos_part, sin_part = phasors(channel[half], np.arange(SECTION), SECTION)
        table[half, 0, :, 0, :] = cos_part
        table[half, 0, :, 1, :] = -sin_part
        table[half, 1, :, 0, :] = sin_part
        table[half, 1, :, 1, :] = cos_part
    return table.reshape(4 * GROUPS, 2 * SECTION)


def two_halves(values):
    high = values.astype(jnp.bfloat16)
    low = (values - high.astype(jnp.float32)).astype(jnp.bfloat16)
    return high, low


def careful_dot(left_high, left_low, right, contract):
    right_high, right_low = two_halves(right)
    dims = (contract, ((), ()))

    def dot(left, values):
        return lax.dot_general(left, values, dims, preferred_element_type=jnp.float32)

    return dot(left_high, right_high) + (dot(left_high, right_low) + dot(left_low, right_high))


def channelize_kernel(
    frame0, frame1, frame2, frame3, frame4, taper,
    outer_high, outer_low, twist_cos, twist_sin, inner_high, inner_low,
    out, strided,
):
    packed_frames = (frame0, frame1, frame2, frame3, frame4)
    columns = []
    for i in range(INPUTS_HERE):
        summed = {}
        for t, packed_ref in enumerate(packed_frames):
            packed = packed_ref[pl.ds(i, OUTER, stride=INPUTS_HERE), :]
            parts = (
                ((packed >> 6) - 32).astype(jnp.float32),
                ((packed & 63) - 32).astype(jnp.float32),
            )
            for f in range(2):
                if 0 <= t - f < TAPS:
                    for part in range(2):
                        term = parts[part] * taper[t - f]
                        key = (f, part)
                        summed[key] = summed[key] + term if key in summed else term
        columns.append(
            jnp.concatenate([summed[f, part] for f in range(2) for part in range(2)], axis=0)
        )
    frames = jnp.concatenate(columns, axis=1)
    first = careful_dot(outer_high[...], outer_low[...], frames, ((1,), (0,)))
    cos_part, sin_part = twist_cos[...], twist_sin[...]
    turned = []
    for i in range(INPUTS_HERE):
        real_part = first[:SECTION, i * SECTION : (i + 1) * SECTION]
        imag_part = first[SECTION:, i * SECTION : (i + 1) * SECTION]
        turned.append(
            jnp.concatenate(
                [
                    real_part * cos_part - imag_part * sin_part,
                    real_part * sin_part + imag_part * cos_part,
                ],
                axis=1,
            )
        )
    turned = jnp.concatenate(turned, axis=0)
    spectra = careful_dot(inner_high[...], inner_low[...], turned, ((1,), (1,)))
    for half in range(2):
        for part in range(2):
            top = (half * 2 + part) * GROUPS
            for i in range(INPUTS_HERE):
                row = half * 8 + i * 2 + part
                strided[pl.ds(row, GROUPS, stride=PAIR_ROWS), :] = spectra[
                    top : top + GROUPS, i * SECTION : (i + 1) * SECTION
                ]
    out[...] = strided[...].astype(jnp.bfloat16).reshape(out.shape)


def channelize_more_kernel(*refs):
    channelize_kernel(*refs[:12], *refs[13:])


def channelize(packed_rows, first_frame, pairs, first_pair, all_pairs, into=None):
    outer_high, outer_low = split_table(outer_table())
    inner_high, inner_low = split_table(inner_table())
    twist_cos, twist_sin = twist_table()
    tables = (pfb_taper(), outer_high, outer_low, twist_cos, twist_sin, inner_high, inner_low)

    def frame_spec(t):
        return pl.BlockSpec((FRAME_ROWS, SECTION), lambda pair: (first_frame + 2 * pair + t, 0))

    def whole(table):
        return pl.BlockSpec(table.shape, lambda pair: (0,) * table.ndim)

    operands = [packed_rows] * 5 + [jnp.asarray(table) for table in tables]
    in_specs = [frame_spec(t) for t in range(5)] + [whole(table) for table in tables]
    kernel, aliases = channelize_kernel, {}
    if into is not None:
        aliases = {len(operands): 0}
        operands.append(into)
        in_specs.append(pl.BlockSpec(memory_space=pl.ANY))
        kernel = channelize_more_kernel
    return pl.pallas_call(
        kernel,
        grid=(pairs,),
        in_specs=in_specs,
        out_specs=pl.BlockSpec(
            (GROUPS, 1, PAIR_ROWS, SECTION), lambda pair: (0, first_pair + pair, 0, 0)
        ),
        out_shape=jax.ShapeDtypeStruct((GROUPS, all_pairs, PAIR_ROWS, SECTION), jnp.bfloat16),
        scratch_shapes=[pltpu.VMEM((GROUPS * PAIR_ROWS, SECTION), jnp.float32)],
        input_output_aliases=aliases,
        compiler_params=pltpu.CompilerParams(vmem_limit_bytes=VMEM_BYTES),
        cost_estimate=pl.CostEstimate(
            flops=pairs * 3 * 2 * 2 * 256 * 256 * 512,
            bytes_accessed=pairs * (5 * 131072 + 262144),
            transcendentals=0,
        ),
        name="channelize",
    )(*operands)


def spread_tables():
    even = np.zeros((INPUTS, INPUTS, 2))
    odd = np.zeros((INPUTS, INPUTS, 2))
    even[np.arange(INPUTS), np.arange(INPUTS), 0] = 1.0
    odd[np.arange(INPUTS), np.arange(INPUTS), 1] = 1.0
    even = even.reshape(INPUTS, 2 * INPUTS)
    odd = odd.reshape(INPUTS, 2 * INPUTS)
    upper = np.concatenate([even, -odd], axis=0)
    lower = np.concatenate([odd, even], axis=0)
    return upper.astype(jnp.bfloat16), lower.astype(jnp.bfloat16)


def weights_kernel(packed_ref, upper, lower, out):
    packed = packed_ref[...]
    parts = jnp.concatenate(
        [
            ((packed >> 6) - 32).astype(jnp.float32).astype(jnp.bfloat16),
            ((packed & 63) - 32).astype(jnp.float32).astype(jnp.bfloat16),
        ],
        axis=1,
    )
    out[:BEAMS] = jnp.dot(parts, upper[...], preferred_element_type=jnp.float32).astype(
        jnp.bfloat16
    )
    out[BEAMS:] = jnp.dot(parts, lower[...], preferred_element_type=jnp.float32).astype(
        jnp.bfloat16
    )


def stacked_weights(packed):
    upper, lower = spread_tables()
    return pl.pallas_call(
        weights_kernel,
        out_shape=jax.ShapeDtypeStruct((2 * BEAMS, 2 * INPUTS), jnp.bfloat16),
        in_specs=[pl.BlockSpec(memory_space=pltpu.VMEM)] * 3,
        out_specs=pl.BlockSpec(memory_space=pltpu.VMEM),
        compiler_params=pltpu.CompilerParams(vmem_limit_bytes=BEAM_VMEM_BYTES),
        cost_estimate=pl.CostEstimate(
            flops=2 * 2 * BEAMS * 512 * 512, bytes_accessed=5 * 2**20, transcendentals=0
        ),
        name="stack_weights",
    )(packed, jnp.asarray(upper), jnp.asarray(lower))


def beam_block(weights_ref, spectra_ref):
    spectra = spectra_ref[...].astype(jnp.float32).reshape(GROUPS, PAIR_ROWS, SECTION)
    paired = jnp.concatenate(
        [
            spectra[:, half * 8 : half * 8 + 8].reshape(2 * INPUTS, SECTION).astype(jnp.bfloat16)
            for half in range(2)
        ],
        axis=1,
    )
    formed = jnp.dot(weights_ref[...], paired, preferred_element_type=jnp.float32)
    real_part, imag_part = formed[:BEAMS], formed[BEAMS:]
    return real_part * real_part + imag_part * imag_part


def beams_kernel(weights_ref, spectra_ref, out, total):
    powers = beam_block(weights_ref, spectra_ref)

    @pl.when(pl.program_id(0) == 0)
    def _():
        total[...] = powers

    @pl.when(pl.program_id(0) > 0)
    def _():
        total[...] += powers

    @pl.when(pl.program_id(0) == pl.num_programs(0) - 1)
    def _():
        scale = 1.0 / (24.0 * math.sqrt(INPUTS)) ** 2 / AVERAGE
        sums = []
        for half in range(2):
            part = total[:, half * SECTION : (half + 1) * SECTION]
            sums.append((part + pltpu.roll(part, OUTER, 1)) * scale)
        lane = lax.broadcasted_iota(jnp.int32, (BEAMS, SECTION), 1)
        out[...] = jnp.where(lane < OUTER, sums[0], sums[1])


def beams(weights, spectra):
    pairs = spectra.shape[1]
    return pl.pallas_call(
        beams_kernel,
        grid=(pairs,),
        in_specs=[
            pl.BlockSpec((2 * BEAMS, 2 * INPUTS), lambda pair: (0, 0)),
            pl.BlockSpec((GROUPS, 1, PAIR_ROWS, SECTION), lambda pair: (0, pair, 0, 0)),
        ],
        out_specs=pl.BlockSpec((BEAMS, SECTION), lambda pair: (0, 0)),
        out_shape=jax.ShapeDtypeStruct((BEAMS, SECTION), jnp.float32),
        scratch_shapes=[pltpu.VMEM((BEAMS, 2 * SECTION), jnp.float32)],
        compiler_params=pltpu.CompilerParams(vmem_limit_bytes=BEAM_VMEM_BYTES),
        cost_estimate=pl.CostEstimate(
            flops=pairs * 2 * 1536 * 512 * 256,
            bytes_accessed=1536 * 512 * 2 + pairs * 262144 + 768 * 128 * 4,
            transcendentals=0,
        ),
        name="beams",
    )(weights, spectra)


EARLY_PAIRS = 2


def per_device(voltages, beam_weights):
    inputs_here, own_len = voltages.shape
    pairs = own_len // CHANNELS // 2
    rows = jnp.transpose(voltages.reshape(inputs_here, own_len // SECTION, SECTION), (1, 0, 2))
    rows = rows.reshape(own_len // SECTION * inputs_here, SECTION)
    rim = (TAPS - 1) * FRAME_ROWS
    devices = lax.axis_size("tm")
    history = lax.ppermute(
        rows[rows.shape[0] - rim :] - ZERO_SAMPLE,
        "tm",
        [(i, i + 1) for i in range(devices - 1)],
    )
    spectra = channelize(
        rows, 2 * EARLY_PAIRS - 3, pairs - EARLY_PAIRS, EARLY_PAIRS, pairs
    )
    early_rows = jnp.concatenate(
        [history + ZERO_SAMPLE, rows[: 2 * EARLY_PAIRS * FRAME_ROWS]], axis=0
    )
    spectra = channelize(early_rows, 0, EARLY_PAIRS, 0, pairs, spectra)
    weights = stacked_weights(beam_weights[0])
    turned = lax.all_to_all(spectra, "chan", 0, 0, tiled=True)
    averaged = beams(weights, turned)
    return lax.all_to_all(averaged[None], "chan", split_axis=1, concat_axis=2, tiled=True)


def solution(mesh):
    return jax.shard_map(
        per_device,
        mesh=mesh,
        in_specs=(P("chan", "tm"), P("chan", None, None)),
        out_specs=P("tm", "chan", None),
        check_vma=False,
    )
```

```python
import functools
import math

import jax
import jax.numpy as jnp
import numpy as np
from jax import lax
from jax.experimental import pallas as pl
from jax.experimental.pallas import tpu as pltpu
from jax.sharding import PartitionSpec as P

INPUTS = 256
BEAMS = 768
CHANNELS = 8192
SECTION = 128
TAPS = 4
AVERAGE = 16
OUTER = 64
GROUPS = 64
ZERO_SAMPLE = 32 * 64 + 32
VMEM_BYTES = 60 * 1024 * 1024
EARLY_VMEM_BYTES = 51 * 1024 * 1024
BEAM_VMEM_BYTES = 51 * 1024 * 1024

INPUTS_HERE = 4
FRAME_ROWS = OUTER * INPUTS_HERE
PAIR_ROWS = 16
EARLY_PAIRS = 2


def split_table(table):
    high = table.astype(jnp.bfloat16)
    low = (table - np.asarray(high, np.float64)).astype(jnp.bfloat16)
    return np.asarray(high), np.asarray(low)


def pfb_taper():
    places = np.arange(TAPS * CHANNELS, dtype=np.float64)
    length = TAPS * CHANNELS
    offsets = (places - 0.5 * length + 0.5) / CHANNELS
    hann_window = 0.5 - 0.5 * np.cos(2.0 * math.pi * (places + 0.5) / length)
    taper = np.sinc(offsets) * hann_window
    return taper.astype(np.float32).reshape(TAPS, OUTER, SECTION)


def phasors(left_index, right_index, length):
    turns = np.outer(left_index, right_index) % length
    angles = turns * (-2.0 * math.pi / length)
    return np.cos(angles), np.sin(angles)


def outer_table():
    cos_part, sin_part = phasors(np.arange(OUTER), np.arange(OUTER), OUTER)
    table = np.zeros((2, 2, OUTER, 2, 2, OUTER))
    for f in range(2):
        table[0, f, :, f, 0, :] = cos_part
        table[0, f, :, f, 1, :] = -sin_part
        table[1, f, :, f, 0, :] = sin_part
        table[1, f, :, f, 1, :] = cos_part
    return table.reshape(4 * OUTER, 4 * OUTER)


def twist_table():
    norm = 1.0 / (32.0 * math.sqrt(CHANNELS))
    cos_part, sin_part = phasors(np.arange(OUTER), np.arange(SECTION), CHANNELS)
    return (
        np.tile(cos_part * norm, (2, 1)).astype(np.float32),
        np.tile(sin_part * norm, (2, 1)).astype(np.float32),
    )


def inner_table():
    channel = np.arange(SECTION).reshape(GROUPS, 2).T
    table = np.zeros((2, 2, GROUPS, 2, SECTION))
    for half in range(2):
        cos_part, sin_part = phasors(channel[half], np.arange(SECTION), SECTION)
        table[half, 0, :, 0, :] = cos_part
        table[half, 0, :, 1, :] = -sin_part
        table[half, 1, :, 0, :] = sin_part
        table[half, 1, :, 1, :] = cos_part
    return table.reshape(4 * GROUPS, 2 * SECTION)


def two_halves(values):
    high = values.astype(jnp.bfloat16)
    low = (values - high.astype(jnp.float32)).astype(jnp.bfloat16)
    return high, low


def careful_dot(left_high, left_low, right, contract):
    right_high, right_low = two_halves(right)
    dims = (contract, ((), ()))

    def dot(left, values):
        return lax.dot_general(left, values, dims, preferred_element_type=jnp.float32)

    return dot(left_high, right_high) + (dot(left_high, right_low) + dot(left_low, right_high))


def channelize_pair(load, tables, waves, strided):
    columns = []
    for i in range(INPUTS_HERE):
        summed = {}
        for t in range(TAPS + 1):
            packed = load(t, i)
            parts = (
                ((packed >> 6) - 32).astype(jnp.float32),
                ((packed & 63) - 32).astype(jnp.float32),
            )
            for f in range(2):
                if 0 <= t - f < TAPS:
                    tap = waves[(t - f) * OUTER : (t - f + 1) * OUTER]
                    for part in range(2):
                        term = parts[part] * tap
                        key = (f, part)
                        summed[key] = summed[key] + term if key in summed else term
        columns.append(
            jnp.concatenate([summed[f, part] for f in range(2) for part in range(2)], axis=0)
        )
    frames = jnp.concatenate(columns, axis=1)
    size = 4 * OUTER
    first = careful_dot(tables[:size], tables[size : 2 * size], frames, ((1,), (0,)))
    cos_part = waves[TAPS * OUTER : TAPS * OUTER + SECTION]
    sin_part = waves[TAPS * OUTER + SECTION : TAPS * OUTER + 2 * SECTION]
    turned = []
    for i in range(INPUTS_HERE):
        real_part = first[:SECTION, i * SECTION : (i + 1) * SECTION]
        imag_part = first[SECTION:, i * SECTION : (i + 1) * SECTION]
        turned.append(
            jnp.concatenate(
                [
                    real_part * cos_part - imag_part * sin_part,
                    real_part * sin_part + imag_part * cos_part,
                ],
                axis=1,
            )
        )
    turned = jnp.concatenate(turned, axis=0)
    spectra = careful_dot(
        tables[2 * size : 3 * size], tables[3 * size : 4 * size], turned, ((1,), (1,))
    )
    for half in range(2):
        for part in range(2):
            top = (half * 2 + part) * GROUPS
            for i in range(INPUTS_HERE):
                row = half * 8 + i * 2 + part
                strided[pl.ds(row, GROUPS, stride=PAIR_ROWS), :] = spectra[
                    top : top + GROUPS, i * SECTION : (i + 1) * SECTION
                ]
    return strided[...].astype(jnp.bfloat16).reshape(GROUPS, PAIR_ROWS, SECTION)


def late_kernel(
    rows, tables_in, waves_in, out,
    frames, tables, waves, strided, staged, frame_sem, table_sem, out_sem,
):
    pairs = staged.shape[0]
    start = (2 * EARLY_PAIRS - (TAPS - 1)) * FRAME_ROWS
    step = 2 * FRAME_ROWS
    lead = (TAPS - 1) * FRAME_ROWS

    def fetch(pair):
        at = 0 if isinstance(pair, int) else lead + pair * step
        size = lead + step if isinstance(pair, int) else step
        return pltpu.make_async_copy(
            rows.at[pl.ds(start + at, size)], frames.at[pl.ds(at, size)], frame_sem.at[pair]
        )

    def send(pair):
        return pltpu.make_async_copy(
            staged.at[pair], out.at[:, EARLY_PAIRS + pair], out_sem.at[pair]
        )

    table_copies = [
        pltpu.make_async_copy(waves_in, waves, table_sem.at[0]),
        pltpu.make_async_copy(tables_in, tables, table_sem.at[1]),
    ]
    table_copies[0].start()
    fetch(0).start()
    table_copies[1].start()

    @pl.loop(1, pairs)
    def _(pair):
        fetch(pair).start()

    for copy in table_copies:
        copy.wait()
    fetch(0).wait()

    @pl.loop(0, pairs)
    def _(pair):
        @pl.when(pair > 0)
        def _():
            fetch(pair).wait()

        def load(t, i):
            return frames[
                pl.ds(pair * step + t * FRAME_ROWS + i, OUTER, stride=INPUTS_HERE), :
            ]

        staged[pair] = channelize_pair(load, tables, waves, strided)
        send(pair).start()

    @pl.loop(0, pairs)
    def _(pair):
        send(pair).wait()


def channelizer_tables():
    outer_high, outer_low = split_table(outer_table())
    inner_high, inner_low = split_table(inner_table())
    twist_cos, twist_sin = twist_table()
    tables = np.concatenate([outer_high, outer_low, inner_high, inner_low], axis=0)
    taper = pfb_taper().reshape(TAPS * OUTER, SECTION)
    waves = np.concatenate([taper, twist_cos, twist_sin], axis=0)
    return jnp.asarray(tables), jnp.asarray(waves)


def channelizer_cost(pairs):
    return pl.CostEstimate(
        flops=pairs * 3 * 2 * 2 * 256 * 256 * 512,
        bytes_accessed=pairs * 2 * 262144 + 2**20,
        transcendentals=0,
    )


def channelize_late(rows, tables, waves, all_pairs):
    pairs = all_pairs - EARLY_PAIRS
    return pl.pallas_call(
        late_kernel,
        in_specs=[pl.BlockSpec(memory_space=pl.ANY)] * 3,
        out_specs=pl.BlockSpec(memory_space=pl.ANY),
        out_shape=jax.ShapeDtypeStruct((GROUPS, all_pairs, PAIR_ROWS, SECTION), jnp.bfloat16),
        scratch_shapes=[
            pltpu.VMEM(((2 * pairs + TAPS - 1) * FRAME_ROWS, SECTION), jnp.int32),
            pltpu.VMEM(tables.shape, tables.dtype),
            pltpu.VMEM(waves.shape, waves.dtype),
            pltpu.VMEM((GROUPS * PAIR_ROWS, SECTION), jnp.float32),
            pltpu.VMEM((pairs, GROUPS, PAIR_ROWS, SECTION), jnp.bfloat16),
            pltpu.SemaphoreType.DMA((pairs,)),
            pltpu.SemaphoreType.DMA((2,)),
            pltpu.SemaphoreType.DMA((pairs,)),
        ],
        compiler_params=pltpu.CompilerParams(vmem_limit_bytes=VMEM_BYTES),
        cost_estimate=channelizer_cost(pairs),
        name="channelize_late",
    )(rows, tables, waves)


def early_kernel(
    history, rows_in, tables, waves, into, out, rows, strided, staged, row_sem, out_sem
):
    rim = TAPS - 1
    fetch = pltpu.make_async_copy(rows_in.at[pl.ds(0, rows.shape[0])], rows, row_sem)
    fetch.start()
    fetch.wait()
    copies = []
    for pair in range(EARLY_PAIRS):

        def load(t, i, pair=pair):
            frame = 2 * pair + t - rim
            if frame < 0:
                at = (frame + rim) * FRAME_ROWS + i
                return history[pl.ds(at, OUTER, stride=INPUTS_HERE), :] + ZERO_SAMPLE
            return rows[pl.ds(frame * FRAME_ROWS + i, OUTER, stride=INPUTS_HERE), :]

        staged[pair] = channelize_pair(load, tables, waves, strided)
        copies.append(pltpu.make_async_copy(staged.at[pair], out.at[:, pair], out_sem.at[pair]))
        copies[-1].start()
    for copy in copies:
        copy.wait()


def channelize_early(history, rows, tables, waves, into):
    near, far = pl.BlockSpec(memory_space=pltpu.VMEM), pl.BlockSpec(memory_space=pl.ANY)
    return pl.pallas_call(
        early_kernel,
        in_specs=[near, far, near, near, far],
        out_specs=far,
        out_shape=jax.ShapeDtypeStruct(into.shape, into.dtype),
        scratch_shapes=[
            pltpu.VMEM((2 * EARLY_PAIRS * FRAME_ROWS, SECTION), jnp.int32),
            pltpu.VMEM((GROUPS * PAIR_ROWS, SECTION), jnp.float32),
            pltpu.VMEM((EARLY_PAIRS, GROUPS, PAIR_ROWS, SECTION), jnp.bfloat16),
            pltpu.SemaphoreType.DMA,
            pltpu.SemaphoreType.DMA((EARLY_PAIRS,)),
        ],
        input_output_aliases={4: 0},
        compiler_params=pltpu.CompilerParams(vmem_limit_bytes=EARLY_VMEM_BYTES),
        cost_estimate=channelizer_cost(EARLY_PAIRS),
        name="channelize_early",
    )(history, rows, tables, waves, into)


def spread_tables():
    even = np.zeros((INPUTS, INPUTS, 2))
    odd = np.zeros((INPUTS, INPUTS, 2))
    even[np.arange(INPUTS), np.arange(INPUTS), 0] = 1.0
    odd[np.arange(INPUTS), np.arange(INPUTS), 1] = 1.0
    even = even.reshape(INPUTS, 2 * INPUTS)
    odd = odd.reshape(INPUTS, 2 * INPUTS)
    upper = np.concatenate([even, -odd], axis=0)
    lower = np.concatenate([odd, even], axis=0)
    return upper.astype(jnp.bfloat16), lower.astype(jnp.bfloat16)


def weights_kernel(packed_ref, upper, lower, out):
    packed = packed_ref[...]
    parts = jnp.concatenate(
        [
            ((packed >> 6) - 32).astype(jnp.float32).astype(jnp.bfloat16),
            ((packed & 63) - 32).astype(jnp.float32).astype(jnp.bfloat16),
        ],
        axis=1,
    )
    out[:BEAMS] = jnp.dot(parts, upper[...], preferred_element_type=jnp.float32).astype(
        jnp.bfloat16
    )
    out[BEAMS:] = jnp.dot(parts, lower[...], preferred_element_type=jnp.float32).astype(
        jnp.bfloat16
    )


def stacked_weights(packed):
    upper, lower = spread_tables()
    tables = (packed, jnp.asarray(upper), jnp.asarray(lower))
    return pl.pallas_call(
        weights_kernel,
        grid=(1,),
        out_shape=jax.ShapeDtypeStruct((2 * BEAMS, 4 * INPUTS), jnp.bfloat16),
        in_specs=[pl.BlockSpec(table.shape, lambda _: (0, 0)) for table in tables],
        out_specs=pl.BlockSpec((2 * BEAMS, 2 * INPUTS), lambda _: (0, 0)),
        compiler_params=pltpu.CompilerParams(vmem_limit_bytes=EARLY_VMEM_BYTES),
        cost_estimate=pl.CostEstimate(
            flops=2 * 2 * BEAMS * 512 * 512, bytes_accessed=5 * 2**20, transcendentals=0
        ),
        name="stack_weights",
    )(*tables)


BEAM_BLOCK = 256


def beams_kernel(weights_in, spectra_ref, out, weights_ref, total, weight_sem):
    pairs = range(spectra_ref.shape[1])
    blocks = range(0, BEAMS, BEAM_BLOCK)

    def fetch_weights(block, part):
        rows = pl.ds(part * BEAMS + block * BEAM_BLOCK, BEAM_BLOCK)
        return pltpu.make_async_copy(
            weights_in.at[rows, pl.ds(0, 2 * INPUTS)], weights_ref.at[rows], weight_sem.at[block, part]
        )

    for block in range(len(blocks)):
        for part in range(2):
            fetch_weights(block, part).start()

    def paired(pair):
        spectra = spectra_ref[:, pair].astype(jnp.float32)
        return jnp.concatenate(
            [
                spectra[:, half * 8 : half * 8 + 8].reshape(2 * INPUTS, SECTION).astype(jnp.bfloat16)
                for half in range(2)
            ],
            axis=1,
        )

    def formed(at, values):
        return jnp.dot(
            weights_ref[at : at + BEAM_BLOCK], values, preferred_element_type=jnp.float32
        )

    values = {}
    for block, at in enumerate(blocks):
        for part in range(2):
            fetch_weights(block, part).wait()
        for pair in pairs:
            if block == 0:
                values[pair] = paired(pair)
            real_part = formed(at, values[pair])
            imag_part = formed(BEAMS + at, values[pair])
            powers = real_part * real_part + imag_part * imag_part
            total[at : at + BEAM_BLOCK] = (
                powers if pair == 0 else total[at : at + BEAM_BLOCK] + powers
            )
    scale = 1.0 / (24.0 * math.sqrt(INPUTS)) ** 2 / AVERAGE
    lane = lax.broadcasted_iota(jnp.int32, (BEAMS, SECTION), 1)
    sums = []
    for half in range(2):
        part = total[:, half * SECTION : (half + 1) * SECTION]
        sums.append((part + pltpu.roll(part, OUTER, 1)) * scale)
    out[...] = jnp.where(lane < OUTER, sums[0], sums[1])


def beams(weights, spectra):
    pairs = spectra.shape[1]
    return pl.pallas_call(
        beams_kernel,
        in_specs=[pl.BlockSpec(memory_space=pl.ANY), pl.BlockSpec(memory_space=pltpu.VMEM)],
        out_specs=pl.BlockSpec(memory_space=pltpu.VMEM),
        out_shape=jax.ShapeDtypeStruct((BEAMS, SECTION), jnp.float32),
        scratch_shapes=[
            pltpu.VMEM((2 * BEAMS, 2 * INPUTS), weights.dtype),
            pltpu.VMEM((BEAMS, 2 * SECTION), jnp.float32),
            pltpu.SemaphoreType.DMA((BEAMS // BEAM_BLOCK, 2)),
        ],
        compiler_params=pltpu.CompilerParams(vmem_limit_bytes=BEAM_VMEM_BYTES),
        cost_estimate=pl.CostEstimate(
            flops=pairs * 2 * 1536 * 512 * 256,
            bytes_accessed=1536 * 512 * 2 + pairs * 262144 + 768 * 128 * 4,
            transcendentals=0,
        ),
        name="beams",
    )(weights, spectra)


def per_device(voltages, beam_weights):
    inputs_here, own_len = voltages.shape
    pairs = own_len // CHANNELS // 2
    rows = jnp.transpose(voltages.reshape(inputs_here, own_len // SECTION, SECTION), (1, 0, 2))
    rows = rows.reshape(own_len // SECTION * inputs_here, SECTION)
    rim = (TAPS - 1) * FRAME_ROWS
    devices = lax.axis_size("tm")
    history = lax.ppermute(
        rows[rows.shape[0] - rim :] - ZERO_SAMPLE,
        "tm",
        [(i, i + 1) for i in range(devices - 1)],
    )
    tables, waves = channelizer_tables()
    spectra = channelize_late(rows, tables, waves, pairs)
    spectra = channelize_early(history, rows, tables, waves, spectra)
    weights = stacked_weights(beam_weights[0])
    turned = lax.all_to_all(spectra, "chan", 0, 0, tiled=True)
    averaged = beams(weights, turned)
    return lax.all_to_all(averaged[None], "chan", split_axis=1, concat_axis=2, tiled=True)


def solution(mesh):
    return jax.shard_map(
        per_device,
        mesh=mesh,
        in_specs=(P("chan", "tm"), P("chan", None, None)),
        out_specs=P("tm", "chan", None),
        check_vma=False,
    )
```

```python
import functools
import math

import jax
import jax.numpy as jnp
import numpy as np
from jax import lax
from jax.experimental import pallas as pl
from jax.experimental.pallas import tpu as pltpu
from jax.sharding import PartitionSpec as P

INPUTS = 256
BEAMS = 768
CHANNELS = 8192
SECTION = 128
TAPS = 4
AVERAGE = 16
OUTER = 64
GROUPS = 64
ZERO_SAMPLE = 32 * 64 + 32
TABLE_ROOM = 6144
LATE_VMEM_BYTES = 51 * 1024 * 1024
EARLY_VMEM_BYTES = 50 * 1024 * 1024
BEAM_VMEM_BYTES = 32 * 1024 * 1024

INPUTS_HERE = 4
FRAME_ROWS = OUTER * INPUTS_HERE
PAIR_ROWS = 16
EARLY_PAIRS = 2


def split_table(table):
    high = table.astype(jnp.bfloat16)
    low = (table - np.asarray(high, np.float64)).astype(jnp.bfloat16)
    return np.asarray(high), np.asarray(low)


def pfb_taper():
    places = np.arange(TAPS * CHANNELS, dtype=np.float64)
    length = TAPS * CHANNELS
    offsets = (places - 0.5 * length + 0.5) / CHANNELS
    hann_window = 0.5 - 0.5 * np.cos(2.0 * math.pi * (places + 0.5) / length)
    taper = np.sinc(offsets) * hann_window
    return taper.astype(np.float32).reshape(TAPS, OUTER, SECTION)


def phasors(left_index, right_index, length):
    turns = np.outer(left_index, right_index) % length
    angles = turns * (-2.0 * math.pi / length)
    return np.cos(angles), np.sin(angles)


def outer_table():
    cos_part, sin_part = phasors(np.arange(OUTER), np.arange(OUTER), OUTER)
    table = np.zeros((2, 2, OUTER, 2, 2, OUTER))
    for f in range(2):
        table[0, f, :, f, 0, :] = cos_part
        table[0, f, :, f, 1, :] = -sin_part
        table[1, f, :, f, 0, :] = sin_part
        table[1, f, :, f, 1, :] = cos_part
    return table.reshape(4 * OUTER, 4 * OUTER)


def twist_table():
    norm = 1.0 / (32.0 * math.sqrt(CHANNELS))
    cos_part, sin_part = phasors(np.arange(OUTER), np.arange(SECTION), CHANNELS)
    return (
        np.tile(cos_part * norm, (2, 1)).astype(np.float32),
        np.tile(sin_part * norm, (2, 1)).astype(np.float32),
    )


def inner_table():
    channel = np.arange(SECTION).reshape(GROUPS, 2).T
    table = np.zeros((2, 2, GROUPS, 2, SECTION))
    for half in range(2):
        cos_part, sin_part = phasors(channel[half], np.arange(SECTION), SECTION)
        table[half, 0, :, 0, :] = cos_part
        table[half, 0, :, 1, :] = -sin_part
        table[half, 1, :, 0, :] = sin_part
        table[half, 1, :, 1, :] = cos_part
    return table.reshape(4 * GROUPS, 2 * SECTION)


def two_halves(values):
    high = values.astype(jnp.bfloat16)
    low = (values - high.astype(jnp.float32)).astype(jnp.bfloat16)
    return high, low


def careful_dot(left_high, left_low, right, contract):
    right_high, right_low = two_halves(right)
    dims = (contract, ((), ()))

    def dot(left, values):
        return lax.dot_general(left, values, dims, preferred_element_type=jnp.float32)

    return dot(left_high, right_high) + (dot(left_high, right_low) + dot(left_low, right_high))


def channelize_pair(load, tables, waves, strided):
    columns = []
    for i in range(INPUTS_HERE):
        summed = {}
        for t in range(TAPS + 1):
            packed = load(t, i)
            parts = (
                ((packed >> 6) - 32).astype(jnp.float32),
                ((packed & 63) - 32).astype(jnp.float32),
            )
            for f in range(2):
                if 0 <= t - f < TAPS:
                    tap = waves[(t - f) * OUTER : (t - f + 1) * OUTER]
                    for part in range(2):
                        term = parts[part] * tap
                        key = (f, part)
                        summed[key] = summed[key] + term if key in summed else term
        columns.append(
            jnp.concatenate([summed[f, part] for f in range(2) for part in range(2)], axis=0)
        )
    frames = jnp.concatenate(columns, axis=1)
    size = 4 * OUTER
    first = careful_dot(tables[:size], tables[size : 2 * size], frames, ((1,), (0,)))
    cos_part = waves[TAPS * OUTER : TAPS * OUTER + SECTION]
    sin_part = waves[TAPS * OUTER + SECTION : TAPS * OUTER + 2 * SECTION]
    turned = []
    for i in range(INPUTS_HERE):
        real_part = first[:SECTION, i * SECTION : (i + 1) * SECTION]
        imag_part = first[SECTION:, i * SECTION : (i + 1) * SECTION]
        turned.append(
            jnp.concatenate(
                [
                    real_part * cos_part - imag_part * sin_part,
                    real_part * sin_part + imag_part * cos_part,
                ],
                axis=1,
            )
        )
    turned = jnp.concatenate(turned, axis=0)
    spectra = careful_dot(
        tables[2 * size : 3 * size], tables[3 * size : 4 * size], turned, ((1,), (1,))
    )
    for half in range(2):
        for part in range(2):
            top = (half * 2 + part) * GROUPS
            for i in range(INPUTS_HERE):
                row = half * 8 + i * 2 + part
                strided[pl.ds(row, GROUPS, stride=PAIR_ROWS), :] = spectra[
                    top : top + GROUPS, i * SECTION : (i + 1) * SECTION
                ]
    return strided[...].astype(jnp.bfloat16).reshape(GROUPS, PAIR_ROWS, SECTION)


def late_kernel(
    rows, tables_in, waves_in, out,
    frames, tables, waves, strided, staged, frame_sem, table_sem, out_sem,
):
    pairs = staged.shape[0]
    start = (2 * EARLY_PAIRS - (TAPS - 1)) * FRAME_ROWS
    step = 2 * FRAME_ROWS
    lead = (TAPS - 1) * FRAME_ROWS

    def fetch(pair):
        at = 0 if isinstance(pair, int) else lead + pair * step
        size = lead + step if isinstance(pair, int) else step
        return pltpu.make_async_copy(
            rows.at[pl.ds(start + at, size)], frames.at[pl.ds(at, size)], frame_sem.at[pair]
        )

    def send(pair):
        return pltpu.make_async_copy(
            staged.at[pair], out.at[:, EARLY_PAIRS + pair], out_sem.at[pair]
        )

    table_copies = [
        pltpu.make_async_copy(waves_in.at[pl.ds(0, waves.shape[0])], waves, table_sem.at[0]),
        pltpu.make_async_copy(tables_in.at[pl.ds(0, tables.shape[0])], tables, table_sem.at[1]),
    ]
    table_copies[0].start()
    fetch(0).start()
    table_copies[1].start()

    @pl.loop(1, pairs)
    def _(pair):
        fetch(pair).start()

    for copy in table_copies:
        copy.wait()
    fetch(0).wait()

    @pl.loop(0, pairs)
    def _(pair):
        @pl.when(pair > 0)
        def _():
            fetch(pair).wait()

        def load(t, i):
            return frames[
                pl.ds(pair * step + t * FRAME_ROWS + i, OUTER, stride=INPUTS_HERE), :
            ]

        staged[pair] = channelize_pair(load, tables, waves, strided)
        send(pair).start()

    @pl.loop(0, pairs)
    def _(pair):
        send(pair).wait()


def channelizer_tables():
    outer_high, outer_low = split_table(outer_table())
    inner_high, inner_low = split_table(inner_table())
    twist_cos, twist_sin = twist_table()
    tables = np.concatenate([outer_high, outer_low, inner_high, inner_low], axis=0)
    taper = pfb_taper().reshape(TAPS * OUTER, SECTION)
    waves = np.concatenate([taper, twist_cos, twist_sin], axis=0)
    return tables, waves


def channelizer_cost(pairs):
    return pl.CostEstimate(
        flops=pairs * 3 * 2 * 2 * 256 * 256 * 512,
        bytes_accessed=pairs * 2 * 262144 + 2**20,
        transcendentals=0,
    )


def channelize_late(rows, tables, waves, all_pairs):
    pairs = all_pairs - EARLY_PAIRS
    padded = [
        jnp.asarray(np.pad(table, ((0, TABLE_ROOM - table.shape[0]), (0, 0))))
        for table in (tables, waves)
    ]
    return pl.pallas_call(
        late_kernel,
        in_specs=[pl.BlockSpec(memory_space=pl.ANY)] * 3,
        out_specs=pl.BlockSpec(memory_space=pl.ANY),
        out_shape=jax.ShapeDtypeStruct((GROUPS, all_pairs, PAIR_ROWS, SECTION), jnp.bfloat16),
        scratch_shapes=[
            pltpu.VMEM(((2 * pairs + TAPS - 1) * FRAME_ROWS, SECTION), jnp.int32),
            pltpu.VMEM(tables.shape, tables.dtype),
            pltpu.VMEM(waves.shape, waves.dtype),
            pltpu.VMEM((GROUPS * PAIR_ROWS, SECTION), jnp.float32),
            pltpu.VMEM((pairs, GROUPS, PAIR_ROWS, SECTION), jnp.bfloat16),
            pltpu.SemaphoreType.DMA((pairs,)),
            pltpu.SemaphoreType.DMA((2,)),
            pltpu.SemaphoreType.DMA((pairs,)),
        ],
        compiler_params=pltpu.CompilerParams(vmem_limit_bytes=LATE_VMEM_BYTES),
        cost_estimate=channelizer_cost(pairs),
        name="channelize_late",
    )(rows, *padded)


def early_kernel(
    history, rows_in, tables, waves, into, out, rows, strided, staged, row_sem, out_sem
):
    rim = TAPS - 1
    fetch = pltpu.make_async_copy(rows_in.at[pl.ds(0, rows.shape[0])], rows, row_sem)
    fetch.start()
    fetch.wait()
    copies = []
    for pair in range(EARLY_PAIRS):

        def load(t, i, pair=pair):
            frame = 2 * pair + t - rim
            if frame < 0:
                at = (frame + rim) * FRAME_ROWS + i
                return history[pl.ds(at, OUTER, stride=INPUTS_HERE), :] + ZERO_SAMPLE
            return rows[pl.ds(frame * FRAME_ROWS + i, OUTER, stride=INPUTS_HERE), :]

        staged[pair] = channelize_pair(load, tables, waves, strided)
        copies.append(pltpu.make_async_copy(staged.at[pair], out.at[:, pair], out_sem.at[pair]))
        copies[-1].start()
    for copy in copies:
        copy.wait()


def channelize_early(history, rows, tables, waves, into):
    near, far = pl.BlockSpec(memory_space=pltpu.VMEM), pl.BlockSpec(memory_space=pl.ANY)
    return pl.pallas_call(
        early_kernel,
        in_specs=[near, far, near, near, far],
        out_specs=far,
        out_shape=jax.ShapeDtypeStruct(into.shape, into.dtype),
        scratch_shapes=[
            pltpu.VMEM((2 * EARLY_PAIRS * FRAME_ROWS, SECTION), jnp.int32),
            pltpu.VMEM((GROUPS * PAIR_ROWS, SECTION), jnp.float32),
            pltpu.VMEM((EARLY_PAIRS, GROUPS, PAIR_ROWS, SECTION), jnp.bfloat16),
            pltpu.SemaphoreType.DMA,
            pltpu.SemaphoreType.DMA((EARLY_PAIRS,)),
        ],
        input_output_aliases={4: 0},
        compiler_params=pltpu.CompilerParams(vmem_limit_bytes=EARLY_VMEM_BYTES),
        cost_estimate=channelizer_cost(EARLY_PAIRS),
        name="channelize_early",
    )(history, rows, jnp.asarray(tables), jnp.asarray(waves), into)


def spread_tables():
    even = np.zeros((INPUTS, INPUTS, 2))
    odd = np.zeros((INPUTS, INPUTS, 2))
    even[np.arange(INPUTS), np.arange(INPUTS), 0] = 1.0
    odd[np.arange(INPUTS), np.arange(INPUTS), 1] = 1.0
    even = even.reshape(INPUTS, 2 * INPUTS)
    odd = odd.reshape(INPUTS, 2 * INPUTS)
    upper = np.concatenate([even, -odd], axis=0)
    lower = np.concatenate([odd, even], axis=0)
    return upper.astype(jnp.bfloat16), lower.astype(jnp.bfloat16)


def weights_kernel(packed_ref, upper, lower, out):
    packed = packed_ref[...]
    parts = jnp.concatenate(
        [
            ((packed >> 6) - 32).astype(jnp.float32).astype(jnp.bfloat16),
            ((packed & 63) - 32).astype(jnp.float32).astype(jnp.bfloat16),
        ],
        axis=1,
    )
    out[:BEAMS] = jnp.dot(parts, upper[...], preferred_element_type=jnp.float32).astype(
        jnp.bfloat16
    )
    out[BEAMS:] = jnp.dot(parts, lower[...], preferred_element_type=jnp.float32).astype(
        jnp.bfloat16
    )


def stacked_weights(packed):
    upper, lower = spread_tables()
    return pl.pallas_call(
        weights_kernel,
        out_shape=jax.ShapeDtypeStruct((2 * BEAMS, 2 * INPUTS), jnp.bfloat16),
        in_specs=[pl.BlockSpec(memory_space=pltpu.VMEM)] * 3,
        out_specs=pl.BlockSpec(memory_space=pltpu.VMEM),
        compiler_params=pltpu.CompilerParams(vmem_limit_bytes=BEAM_VMEM_BYTES),
        cost_estimate=pl.CostEstimate(
            flops=2 * 2 * BEAMS * 512 * 512, bytes_accessed=5 * 2**20, transcendentals=0
        ),
        name="stack_weights",
    )(packed, jnp.asarray(upper), jnp.asarray(lower))


BEAM_BLOCK = 256


def beams_kernel(weights_ref, spectra_ref, out, total):
    pairs = range(spectra_ref.shape[1])
    blocks = range(0, BEAMS, BEAM_BLOCK)

    def paired(pair):
        spectra = spectra_ref[:, pair].astype(jnp.float32)
        return jnp.concatenate(
            [
                spectra[:, half * 8 : half * 8 + 8].reshape(2 * INPUTS, SECTION).astype(jnp.bfloat16)
                for half in range(2)
            ],
            axis=1,
        )

    def formed(at, values):
        return jnp.dot(
            weights_ref[at : at + BEAM_BLOCK], values, preferred_element_type=jnp.float32
        )

    values = {}
    for block, at in enumerate(blocks):
        for pair in pairs:
            if block == 0:
                values[pair] = paired(pair)
            real_part = formed(at, values[pair])
            imag_part = formed(BEAMS + at, values[pair])
            powers = real_part * real_part + imag_part * imag_part
            total[at : at + BEAM_BLOCK] = (
                powers if pair == 0 else total[at : at + BEAM_BLOCK] + powers
            )
    scale = 1.0 / (24.0 * math.sqrt(INPUTS)) ** 2 / AVERAGE
    lane = lax.broadcasted_iota(jnp.int32, (BEAMS, SECTION), 1)
    sums = []
    for half in range(2):
        part = total[:, half * SECTION : (half + 1) * SECTION]
        sums.append((part + pltpu.roll(part, OUTER, 1)) * scale)
    out[...] = jnp.where(lane < OUTER, sums[0], sums[1])


def beams(weights, spectra):
    pairs = spectra.shape[1]
    return pl.pallas_call(
        beams_kernel,
        in_specs=[pl.BlockSpec(memory_space=pltpu.VMEM)] * 2,
        out_specs=pl.BlockSpec(memory_space=pltpu.VMEM),
        out_shape=jax.ShapeDtypeStruct((BEAMS, SECTION), jnp.float32),
        scratch_shapes=[pltpu.VMEM((BEAMS, 2 * SECTION), jnp.float32)],
        compiler_params=pltpu.CompilerParams(vmem_limit_bytes=BEAM_VMEM_BYTES),
        cost_estimate=pl.CostEstimate(
            flops=pairs * 2 * 1536 * 512 * 256,
            bytes_accessed=1536 * 512 * 2 + pairs * 262144 + 768 * 128 * 4,
            transcendentals=0,
        ),
        name="beams",
    )(weights, spectra)


def per_device(voltages, beam_weights):
    inputs_here, own_len = voltages.shape
    pairs = own_len // CHANNELS // 2
    rows = jnp.transpose(voltages.reshape(inputs_here, own_len // SECTION, SECTION), (1, 0, 2))
    rows = rows.reshape(own_len // SECTION * inputs_here, SECTION)
    rim = (TAPS - 1) * FRAME_ROWS
    devices = lax.axis_size("tm")
    history = lax.ppermute(
        rows[rows.shape[0] - rim :] - ZERO_SAMPLE,
        "tm",
        [(i, i + 1) for i in range(devices - 1)],
    )
    tables, waves = channelizer_tables()
    spectra = channelize_late(rows, tables, waves, pairs)
    spectra, packed_weights = lax.optimization_barrier((spectra, beam_weights[0]))
    weights = stacked_weights(packed_weights)
    spectra = channelize_early(history, rows, tables, waves, spectra)
    spectra, weights = lax.optimization_barrier((spectra, weights))
    turned = lax.all_to_all(spectra, "chan", 0, 0, tiled=True)
    averaged = beams(weights, turned)
    return lax.all_to_all(averaged[None], "chan", split_axis=1, concat_axis=2, tiled=True)


def solution(mesh):
    return jax.shard_map(
        per_device,
        mesh=mesh,
        in_specs=(P("chan", "tm"), P("chan", None, None)),
        out_specs=P("tm", "chan", None),
        check_vma=False,
    )
```

```python
import functools
import math

import jax
import jax.numpy as jnp
import numpy as np
from jax import lax
from jax.experimental import pallas as pl
from jax.experimental.pallas import tpu as pltpu
from jax.sharding import PartitionSpec as P

INPUTS = 256
BEAMS = 768
CHANNELS = 8192
SECTION = 128
TAPS = 4
AVERAGE = 16
OUTER = 64
GROUPS = 64
ZERO_SAMPLE = 32 * 64 + 32
TABLE_ROOM = 6144
LATE_VMEM_BYTES = 51 * 1024 * 1024
EARLY_VMEM_BYTES = 50 * 1024 * 1024
BEAM_VMEM_BYTES = 32 * 1024 * 1024

INPUTS_HERE = 4
FRAME_ROWS = OUTER * INPUTS_HERE
PAIR_ROWS = 16
EARLY_PAIRS = 2


def split_table(table):
    high = table.astype(jnp.bfloat16)
    low = (table - np.asarray(high, np.float64)).astype(jnp.bfloat16)
    return np.asarray(high), np.asarray(low)


def pfb_taper():
    places = np.arange(TAPS * CHANNELS, dtype=np.float64)
    length = TAPS * CHANNELS
    offsets = (places - 0.5 * length + 0.5) / CHANNELS
    hann_window = 0.5 - 0.5 * np.cos(2.0 * math.pi * (places + 0.5) / length)
    taper = np.sinc(offsets) * hann_window
    return taper.astype(np.float32).reshape(TAPS, OUTER, SECTION)


def phasors(left_index, right_index, length):
    turns = np.outer(left_index, right_index) % length
    angles = turns * (-2.0 * math.pi / length)
    return np.cos(angles), np.sin(angles)


def outer_table():
    cos_part, sin_part = phasors(np.arange(OUTER), np.arange(OUTER), OUTER)
    table = np.zeros((2, 2, OUTER, 2, 2, OUTER))
    for f in range(2):
        table[0, f, :, f, 0, :] = cos_part
        table[0, f, :, f, 1, :] = -sin_part
        table[1, f, :, f, 0, :] = sin_part
        table[1, f, :, f, 1, :] = cos_part
    return table.reshape(4 * OUTER, 4 * OUTER)


def twist_table():
    norm = 1.0 / (32.0 * math.sqrt(CHANNELS))
    cos_part, sin_part = phasors(np.arange(OUTER), np.arange(SECTION), CHANNELS)
    return (
        np.tile(cos_part * norm, (2, 1)).astype(np.float32),
        np.tile(sin_part * norm, (2, 1)).astype(np.float32),
    )


def inner_table():
    channel = np.arange(SECTION).reshape(GROUPS, 2).T
    table = np.zeros((2, 2, GROUPS, 2, SECTION))
    for half in range(2):
        cos_part, sin_part = phasors(channel[half], np.arange(SECTION), SECTION)
        table[half, 0, :, 0, :] = cos_part
        table[half, 0, :, 1, :] = -sin_part
        table[half, 1, :, 0, :] = sin_part
        table[half, 1, :, 1, :] = cos_part
    return table.reshape(4 * GROUPS, 2 * SECTION)


def two_halves(values):
    high = values.astype(jnp.bfloat16)
    low = (values - high.astype(jnp.float32)).astype(jnp.bfloat16)
    return high, low


def careful_dot(left_high, left_low, right, contract):
    right_high, right_low = two_halves(right)
    dims = (contract, ((), ()))

    def dot(left, values):
        return lax.dot_general(left, values, dims, preferred_element_type=jnp.float32)

    return dot(left_high, right_high) + (dot(left_high, right_low) + dot(left_low, right_high))


def filtered(load, waves, inputs):
    columns = []
    for i in inputs:
        summed = {}
        for t in range(TAPS + 1):
            packed = load(t, i)
            parts = (
                ((packed >> 6) - 32).astype(jnp.float32),
                ((packed & 63) - 32).astype(jnp.float32),
            )
            for f in range(2):
                if 0 <= t - f < TAPS:
                    tap = waves[(t - f) * OUTER : (t - f + 1) * OUTER]
                    for part in range(2):
                        term = parts[part] * tap
                        key = (f, part)
                        summed[key] = summed[key] + term if key in summed else term
        columns.append(
            jnp.concatenate([summed[f, part] for f in range(2) for part in range(2)], axis=0)
        )
    return jnp.concatenate(columns, axis=1)


def twisted(first, waves, count):
    cos_part = waves[TAPS * OUTER : TAPS * OUTER + SECTION]
    sin_part = waves[TAPS * OUTER + SECTION : TAPS * OUTER + 2 * SECTION]
    turned = []
    for i in range(count):
        real_part = first[:SECTION, i * SECTION : (i + 1) * SECTION]
        imag_part = first[SECTION:, i * SECTION : (i + 1) * SECTION]
        turned.append(
            jnp.concatenate(
                [
                    real_part * cos_part - imag_part * sin_part,
                    real_part * sin_part + imag_part * cos_part,
                ],
                axis=1,
            )
        )
    return jnp.concatenate(turned, axis=0)


def interleave(spectra, inputs, strided):
    for half in range(2):
        for part in range(2):
            top = (half * 2 + part) * GROUPS
            for at, i in enumerate(inputs):
                row = half * 8 + i * 2 + part
                strided[pl.ds(row, GROUPS, stride=PAIR_ROWS), :] = spectra[
                    top : top + GROUPS, at * SECTION : (at + 1) * SECTION
                ]


def channelize_pairs(loads, tables, waves, strided, finish):
    size = 4 * OUTER
    sets = [(0, 1), (2, 3)]
    steps = [(pair, inputs) for pair in range(len(loads)) for inputs in sets]
    frames = filtered(loads[0], waves, sets[0])
    for number, (pair, inputs) in enumerate(steps):
        first = careful_dot(tables[:size], tables[size : 2 * size], frames, ((1,), (0,)))
        if number + 1 < len(steps):
            next_pair, next_inputs = steps[number + 1]
            frames = filtered(loads[next_pair], waves, next_inputs)
        turned = twisted(first, waves, len(inputs))
        spectra = careful_dot(
            tables[2 * size : 3 * size], tables[3 * size : 4 * size], turned, ((1,), (1,))
        )
        interleave(spectra, inputs, strided.at[pair])
        if inputs == sets[-1]:
            finish(pair, strided[pair].astype(jnp.bfloat16).reshape(GROUPS, PAIR_ROWS, SECTION))


def late_kernel(
    rows, tables_in, waves_in, out, head,
    frames, tables, waves, strided, staged, frame_sem, table_sem, out_sem, head_sem,
):
    pairs = staged.shape[0]
    start = (2 * EARLY_PAIRS - (TAPS - 1)) * FRAME_ROWS
    step = 2 * FRAME_ROWS
    lead = (TAPS - 1) * FRAME_ROWS

    def fetch(pair):
        at = 0 if isinstance(pair, int) else lead + pair * step
        size = lead + step if isinstance(pair, int) else step
        return pltpu.make_async_copy(
            rows.at[pl.ds(start + at, size)], frames.at[pl.ds(at, size)], frame_sem.at[pair]
        )

    def send(pair):
        return pltpu.make_async_copy(
            staged.at[pair], out.at[:, EARLY_PAIRS + pair], out_sem.at[pair]
        )

    table_copies = [
        pltpu.make_async_copy(waves_in.at[pl.ds(0, waves.shape[0])], waves, table_sem.at[0]),
        pltpu.make_async_copy(tables_in.at[pl.ds(0, tables.shape[0])], tables, table_sem.at[1]),
    ]
    table_copies[0].start()
    fetch(0).start()
    table_copies[1].start()

    @pl.loop(1, pairs)
    def _(pair):
        fetch(pair).start()

    head_copy = pltpu.make_async_copy(rows.at[pl.ds(0, head.shape[0])], head, head_sem)
    head_copy.start()
    for copy in table_copies:
        copy.wait()
    fetch(0).wait()

    @pl.loop(1, pairs)
    def _(pair):
        fetch(pair).wait()

    def loader(pair):
        def load(t, i):
            at = pair * step + t * FRAME_ROWS + i
            return frames[pl.ds(at, OUTER, stride=INPUTS_HERE), :]

        return load

    def finish(pair, spectra):
        staged[pair] = spectra
        send(pair).start()

    channelize_pairs([loader(pair) for pair in range(pairs)], tables, waves, strided, finish)
    head_copy.wait()
    for pair in range(pairs):
        send(pair).wait()


def channelizer_tables():
    outer_high, outer_low = split_table(outer_table())
    inner_high, inner_low = split_table(inner_table())
    twist_cos, twist_sin = twist_table()
    tables = np.concatenate([outer_high, outer_low, inner_high, inner_low], axis=0)
    taper = pfb_taper().reshape(TAPS * OUTER, SECTION)
    waves = np.concatenate([taper, twist_cos, twist_sin], axis=0)
    return tables, waves


def channelizer_cost(pairs):
    return pl.CostEstimate(
        flops=pairs * 3 * 2 * 2 * 256 * 256 * 512,
        bytes_accessed=pairs * 2 * 262144 + 2**20,
        transcendentals=0,
    )


def channelize_late(rows, tables, waves, all_pairs):
    pairs = all_pairs - EARLY_PAIRS
    padded = [
        jnp.asarray(np.pad(table, ((0, TABLE_ROOM - table.shape[0]), (0, 0))))
        for table in (tables, waves)
    ]
    return pl.pallas_call(
        late_kernel,
        in_specs=[pl.BlockSpec(memory_space=pl.ANY)] * 3,
        out_specs=[pl.BlockSpec(memory_space=pl.ANY)] * 2,
        out_shape=[
            jax.ShapeDtypeStruct((GROUPS, all_pairs, PAIR_ROWS, SECTION), jnp.bfloat16),
            jax.ShapeDtypeStruct((2 * EARLY_PAIRS * FRAME_ROWS, SECTION), rows.dtype),
        ],
        scratch_shapes=[
            pltpu.VMEM(((2 * pairs + TAPS - 1) * FRAME_ROWS, SECTION), jnp.int32),
            pltpu.VMEM(tables.shape, tables.dtype),
            pltpu.VMEM(waves.shape, waves.dtype),
            pltpu.VMEM((pairs, GROUPS * PAIR_ROWS, SECTION), jnp.float32),
            pltpu.VMEM((pairs, GROUPS, PAIR_ROWS, SECTION), jnp.bfloat16),
            pltpu.SemaphoreType.DMA((pairs,)),
            pltpu.SemaphoreType.DMA((2,)),
            pltpu.SemaphoreType.DMA((pairs,)),
            pltpu.SemaphoreType.DMA,
        ],
        compiler_params=pltpu.CompilerParams(vmem_limit_bytes=LATE_VMEM_BYTES),
        cost_estimate=channelizer_cost(pairs),
        name="channelize_late",
    )(rows, *padded)


def early_kernel(history, rows, tables, waves, into, out, strided, staged, out_sem):
    rim = TAPS - 1

    def send(pair):
        return pltpu.make_async_copy(staged.at[pair], out.at[:, pair], out_sem.at[pair])

    def loader(pair):
        def load(t, i):
            frame = 2 * pair + t - rim
            if frame < 0:
                at = (frame + rim) * FRAME_ROWS + i
                return history[pl.ds(at, OUTER, stride=INPUTS_HERE), :] + ZERO_SAMPLE
            return rows[pl.ds(frame * FRAME_ROWS + i, OUTER, stride=INPUTS_HERE), :]

        return load

    def finish(pair, spectra):
        staged[pair] = spectra
        send(pair).start()

    channelize_pairs(
        [loader(pair) for pair in range(EARLY_PAIRS)], tables, waves, strided, finish
    )
    for pair in range(EARLY_PAIRS):
        send(pair).wait()


def channelize_early(history, rows, tables, waves, into):
    near, far = pl.BlockSpec(memory_space=pltpu.VMEM), pl.BlockSpec(memory_space=pl.ANY)
    return pl.pallas_call(
        early_kernel,
        in_specs=[near, near, near, near, far],
        out_specs=far,
        out_shape=jax.ShapeDtypeStruct(into.shape, into.dtype),
        scratch_shapes=[
            pltpu.VMEM((EARLY_PAIRS, GROUPS * PAIR_ROWS, SECTION), jnp.float32),
            pltpu.VMEM((EARLY_PAIRS, GROUPS, PAIR_ROWS, SECTION), jnp.bfloat16),
            pltpu.SemaphoreType.DMA((EARLY_PAIRS,)),
        ],
        input_output_aliases={4: 0},
        compiler_params=pltpu.CompilerParams(vmem_limit_bytes=EARLY_VMEM_BYTES),
        cost_estimate=channelizer_cost(EARLY_PAIRS),
        name="channelize_early",
    )(history, rows, jnp.asarray(tables), jnp.asarray(waves), into)


def spread_tables():
    even = np.zeros((INPUTS, INPUTS, 2))
    odd = np.zeros((INPUTS, INPUTS, 2))
    even[np.arange(INPUTS), np.arange(INPUTS), 0] = 1.0
    odd[np.arange(INPUTS), np.arange(INPUTS), 1] = 1.0
    even = even.reshape(INPUTS, 2 * INPUTS)
    odd = odd.reshape(INPUTS, 2 * INPUTS)
    upper = np.concatenate([even, -odd], axis=0)
    lower = np.concatenate([odd, even], axis=0)
    return upper.astype(jnp.bfloat16), lower.astype(jnp.bfloat16)


def weights_kernel(packed_ref, upper, lower, out):
    packed = packed_ref[...]
    parts = jnp.concatenate(
        [
            ((packed >> 6) - 32).astype(jnp.float32).astype(jnp.bfloat16),
            ((packed & 63) - 32).astype(jnp.float32).astype(jnp.bfloat16),
        ],
        axis=1,
    )
    out[:BEAMS] = jnp.dot(parts, upper[...], preferred_element_type=jnp.float32).astype(
        jnp.bfloat16
    )
    out[BEAMS:] = jnp.dot(parts, lower[...], preferred_element_type=jnp.float32).astype(
        jnp.bfloat16
    )


def stacked_weights(packed):
    upper, lower = spread_tables()
    return pl.pallas_call(
        weights_kernel,
        out_shape=jax.ShapeDtypeStruct((2 * BEAMS, 2 * INPUTS), jnp.bfloat16),
        in_specs=[pl.BlockSpec(memory_space=pltpu.VMEM)] * 3,
        out_specs=pl.BlockSpec(memory_space=pltpu.VMEM),
        compiler_params=pltpu.CompilerParams(vmem_limit_bytes=BEAM_VMEM_BYTES),
        cost_estimate=pl.CostEstimate(
            flops=2 * 2 * BEAMS * 512 * 512, bytes_accessed=5 * 2**20, transcendentals=0
        ),
        name="stack_weights",
    )(packed, jnp.asarray(upper), jnp.asarray(lower))


BEAM_BLOCK = 256


def beams_kernel(weights_ref, spectra_ref, out, total):
    pairs = range(spectra_ref.shape[1])
    blocks = range(0, BEAMS, BEAM_BLOCK)

    def paired(pair):
        spectra = spectra_ref[:, pair].astype(jnp.float32)
        return jnp.concatenate(
            [
                spectra[:, half * 8 : half * 8 + 8].reshape(2 * INPUTS, SECTION).astype(jnp.bfloat16)
                for half in range(2)
            ],
            axis=1,
        )

    def formed(at, values):
        return jnp.dot(
            weights_ref[at : at + BEAM_BLOCK], values, preferred_element_type=jnp.float32
        )

    values = {}
    for block, at in enumerate(blocks):
        for pair in pairs:
            if block == 0:
                values[pair] = paired(pair)
            real_part = formed(at, values[pair])
            imag_part = formed(BEAMS + at, values[pair])
            powers = real_part * real_part + imag_part * imag_part
            total[at : at + BEAM_BLOCK] = (
                powers if pair == 0 else total[at : at + BEAM_BLOCK] + powers
            )
    scale = 1.0 / (24.0 * math.sqrt(INPUTS)) ** 2 / AVERAGE
    lane = lax.broadcasted_iota(jnp.int32, (BEAMS, SECTION), 1)
    sums = []
    for half in range(2):
        part = total[:, half * SECTION : (half + 1) * SECTION]
        sums.append((part + pltpu.roll(part, OUTER, 1)) * scale)
    out[...] = jnp.where(lane < OUTER, sums[0], sums[1])


def beams(weights, spectra):
    pairs = spectra.shape[1]
    return pl.pallas_call(
        beams_kernel,
        in_specs=[pl.BlockSpec(memory_space=pltpu.VMEM)] * 2,
        out_specs=pl.BlockSpec(memory_space=pltpu.VMEM),
        out_shape=jax.ShapeDtypeStruct((BEAMS, SECTION), jnp.float32),
        scratch_shapes=[pltpu.VMEM((BEAMS, 2 * SECTION), jnp.float32)],
        compiler_params=pltpu.CompilerParams(vmem_limit_bytes=BEAM_VMEM_BYTES),
        cost_estimate=pl.CostEstimate(
            flops=pairs * 2 * 1536 * 512 * 256,
            bytes_accessed=1536 * 512 * 2 + pairs * 262144 + 768 * 128 * 4,
            transcendentals=0,
        ),
        name="beams",
    )(weights, spectra)


def per_device(voltages, beam_weights):
    inputs_here, own_len = voltages.shape
    pairs = own_len // CHANNELS // 2
    rows = jnp.transpose(voltages.reshape(inputs_here, own_len // SECTION, SECTION), (1, 0, 2))
    rows = rows.reshape(own_len // SECTION * inputs_here, SECTION)
    rim = (TAPS - 1) * FRAME_ROWS
    devices = lax.axis_size("tm")
    history = lax.ppermute(
        rows[rows.shape[0] - rim :] - ZERO_SAMPLE,
        "tm",
        [(i, i + 1) for i in range(devices - 1)],
    )
    tables, waves = channelizer_tables()
    spectra, head = channelize_late(rows, tables, waves, pairs)
    spectra, packed_weights = lax.optimization_barrier((spectra, beam_weights[0]))
    weights = stacked_weights(packed_weights)
    spectra = channelize_early(history, head, tables, waves, spectra)
    spectra, weights = lax.optimization_barrier((spectra, weights))
    turned = lax.all_to_all(spectra, "chan", 0, 0, tiled=True)
    averaged = beams(weights, turned)
    return lax.all_to_all(averaged[None], "chan", split_axis=1, concat_axis=2, tiled=True)


def solution(mesh):
    return jax.shard_map(
        per_device,
        mesh=mesh,
        in_specs=(P("chan", "tm"), P("chan", None, None)),
        out_specs=P("tm", "chan", None),
        check_vma=False,
    )
```

```python
import functools
import math

import jax
import jax.numpy as jnp
import numpy as np
from jax import lax
from jax.experimental import pallas as pl
from jax.experimental.pallas import tpu as pltpu
from jax.sharding import PartitionSpec as P

INPUTS = 256
BEAMS = 768
CHANNELS = 8192
SECTION = 128
TAPS = 4
AVERAGE = 16
OUTER = 64
GROUPS = 64
ZERO_SAMPLE = 32 * 64 + 32
TABLE_ROOM = 6144
LATE_VMEM_BYTES = 51 * 1024 * 1024
EARLY_VMEM_BYTES = 50 * 1024 * 1024
BEAM_VMEM_BYTES = 32 * 1024 * 1024

INPUTS_HERE = 4
FRAME_ROWS = OUTER * INPUTS_HERE
PAIR_ROWS = 16
EARLY_PAIRS = 2
ORDER = [
    4, 47, 59, 35, 43, 22, 6, 18, 60, 56, 24, 20, 44, 34, 63, 10,
    7, 54, 5, 57, 33, 19, 8, 48, 13, 27, 17, 45, 62, 26, 55, 40,
    16, 2, 37, 41, 11, 14, 46, 25, 32, 36, 21, 23, 30, 29, 53, 38,
    3, 1, 51, 50, 61, 0, 52, 28, 49, 31, 15, 39, 9, 42, 12, 58,
]


def split_table(table):
    high = table.astype(jnp.bfloat16)
    low = (table - np.asarray(high, np.float64)).astype(jnp.bfloat16)
    return np.asarray(high), np.asarray(low)


def pfb_taper():
    places = np.arange(TAPS * CHANNELS, dtype=np.float64)
    length = TAPS * CHANNELS
    offsets = (places - 0.5 * length + 0.5) / CHANNELS
    hann_window = 0.5 - 0.5 * np.cos(2.0 * math.pi * (places + 0.5) / length)
    taper = np.sinc(offsets) * hann_window
    return taper.astype(np.float32).reshape(TAPS, OUTER, SECTION)


def phasors(left_index, right_index, length):
    turns = np.outer(left_index, right_index) % length
    angles = turns * (-2.0 * math.pi / length)
    return np.cos(angles), np.sin(angles)


def outer_table():
    cos_part, sin_part = phasors(np.arange(OUTER), np.arange(OUTER), OUTER)
    table = np.zeros((2, 2, OUTER, 2, 2, OUTER))
    for f in range(2):
        table[0, f, :, f, 0, :] = cos_part
        table[0, f, :, f, 1, :] = -sin_part
        table[1, f, :, f, 0, :] = sin_part
        table[1, f, :, f, 1, :] = cos_part
    return table.reshape(4 * OUTER, 4 * OUTER)


def twist_table():
    norm = 1.0 / (32.0 * math.sqrt(CHANNELS))
    cos_part, sin_part = phasors(np.arange(OUTER), np.arange(SECTION), CHANNELS)
    return (
        np.tile(cos_part * norm, (2, 1)).astype(np.float32),
        np.tile(sin_part * norm, (2, 1)).astype(np.float32),
    )


def inner_table():
    channel = np.arange(SECTION).reshape(GROUPS, 2)[ORDER].T
    table = np.zeros((2, 2, GROUPS, 2, SECTION))
    for half in range(2):
        cos_part, sin_part = phasors(channel[half], np.arange(SECTION), SECTION)
        table[half, 0, :, 0, :] = cos_part
        table[half, 0, :, 1, :] = -sin_part
        table[half, 1, :, 0, :] = sin_part
        table[half, 1, :, 1, :] = cos_part
    return table.reshape(4 * GROUPS, 2 * SECTION)


def two_halves(values):
    high = values.astype(jnp.bfloat16)
    low = (values - high.astype(jnp.float32)).astype(jnp.bfloat16)
    return high, low


def careful_dot(left_high, left_low, right, contract):
    right_high, right_low = two_halves(right)
    dims = (contract, ((), ()))

    def dot(left, values):
        return lax.dot_general(left, values, dims, preferred_element_type=jnp.float32)

    return dot(left_high, right_high) + (dot(left_high, right_low) + dot(left_low, right_high))


def filtered(load, waves, inputs):
    columns = []
    for i in inputs:
        summed = {}
        for t in range(TAPS + 1):
            packed = load(t, i)
            parts = (
                ((packed >> 6) - 32).astype(jnp.float32),
                ((packed & 63) - 32).astype(jnp.float32),
            )
            for f in range(2):
                if 0 <= t - f < TAPS:
                    tap = waves[(t - f) * OUTER : (t - f + 1) * OUTER]
                    for part in range(2):
                        term = parts[part] * tap
                        key = (f, part)
                        summed[key] = summed[key] + term if key in summed else term
        columns.append(
            jnp.concatenate([summed[f, part] for f in range(2) for part in range(2)], axis=0)
        )
    return jnp.concatenate(columns, axis=1)


def twisted(first, waves, count):
    cos_part = waves[TAPS * OUTER : TAPS * OUTER + SECTION]
    sin_part = waves[TAPS * OUTER + SECTION : TAPS * OUTER + 2 * SECTION]
    turned = []
    for i in range(count):
        real_part = first[:SECTION, i * SECTION : (i + 1) * SECTION]
        imag_part = first[SECTION:, i * SECTION : (i + 1) * SECTION]
        turned.append(
            jnp.concatenate(
                [
                    real_part * cos_part - imag_part * sin_part,
                    real_part * sin_part + imag_part * cos_part,
                ],
                axis=1,
            )
        )
    return jnp.concatenate(turned, axis=0)


def interleave(spectra, inputs, strided):
    for half in range(2):
        for part in range(2):
            top = (half * 2 + part) * GROUPS
            for at, i in enumerate(inputs):
                row = half * 8 + i * 2 + part
                strided[pl.ds(row, GROUPS, stride=PAIR_ROWS), :] = spectra[
                    top : top + GROUPS, at * SECTION : (at + 1) * SECTION
                ]


def channelize_pairs(loads, tables, waves, strided, finish):
    size = 4 * OUTER
    sets = [(0, 1), (2, 3)]
    steps = [(pair, inputs) for pair in range(len(loads)) for inputs in sets]
    frames = filtered(loads[0], waves, sets[0])
    for number, (pair, inputs) in enumerate(steps):
        first = careful_dot(tables[:size], tables[size : 2 * size], frames, ((1,), (0,)))
        if number + 1 < len(steps):
            next_pair, next_inputs = steps[number + 1]
            frames = filtered(loads[next_pair], waves, next_inputs)
        turned = twisted(first, waves, len(inputs))
        spectra = careful_dot(
            tables[2 * size : 3 * size], tables[3 * size : 4 * size], turned, ((1,), (1,))
        )
        interleave(spectra, inputs, strided.at[pair])
        if inputs == sets[-1]:
            finish(pair, strided[pair].astype(jnp.bfloat16).reshape(GROUPS, PAIR_ROWS, SECTION))


def late_kernel(
    rows, tables_in, waves_in, out, head,
    frames, tables, waves, strided, frame_sem, table_sem, head_sem,
):
    pairs = frame_sem.shape[0]
    start = (2 * EARLY_PAIRS - (TAPS - 1)) * FRAME_ROWS
    step = 2 * FRAME_ROWS
    lead = (TAPS - 1) * FRAME_ROWS

    def fetch(pair):
        at = 0 if isinstance(pair, int) else lead + pair * step
        size = lead + step if isinstance(pair, int) else step
        return pltpu.make_async_copy(
            rows.at[pl.ds(start + at, size)], frames.at[pl.ds(at, size)], frame_sem.at[pair]
        )

    table_copies = [
        pltpu.make_async_copy(waves_in.at[pl.ds(0, waves.shape[0])], waves, table_sem.at[0]),
        pltpu.make_async_copy(tables_in.at[pl.ds(0, tables.shape[0])], tables, table_sem.at[1]),
    ]
    table_copies[0].start()
    fetch(0).start()
    table_copies[1].start()

    @pl.loop(1, pairs)
    def _(pair):
        fetch(pair).start()

    head_copy = pltpu.make_async_copy(rows.at[pl.ds(0, head.shape[0])], head, head_sem)
    head_copy.start()
    for copy in table_copies:
        copy.wait()
    fetch(0).wait()

    @pl.loop(1, pairs)
    def _(pair):
        fetch(pair).wait()

    def loader(pair):
        def load(t, i):
            at = pair * step + t * FRAME_ROWS + i
            return frames[pl.ds(at, OUTER, stride=INPUTS_HERE), :]

        return load

    @pl.loop(0, pairs // 3)
    def _(turn):
        def finish(pair, spectra):
            out[:, EARLY_PAIRS + turn * 3 + pair] = spectra

        loads = [loader(turn * 3 + pair) for pair in range(3)]
        channelize_pairs(loads, tables, waves, strided, finish)

    head_copy.wait()


def channelizer_tables():
    outer_high, outer_low = split_table(outer_table())
    inner_high, inner_low = split_table(inner_table())
    twist_cos, twist_sin = twist_table()
    tables = np.concatenate([outer_high, outer_low, inner_high, inner_low], axis=0)
    taper = pfb_taper().reshape(TAPS * OUTER, SECTION)
    waves = np.concatenate([taper, twist_cos, twist_sin], axis=0)
    return tables, waves


def channelizer_cost(pairs):
    return pl.CostEstimate(
        flops=pairs * 3 * 2 * 2 * 256 * 256 * 512,
        bytes_accessed=pairs * 2 * 262144 + 2**20,
        transcendentals=0,
    )


def channelize_late(rows, tables, waves, all_pairs):
    pairs = all_pairs - EARLY_PAIRS
    padded = [
        jnp.asarray(np.pad(table, ((0, TABLE_ROOM - table.shape[0]), (0, 0))))
        for table in (tables, waves)
    ]
    return pl.pallas_call(
        late_kernel,
        in_specs=[pl.BlockSpec(memory_space=pl.ANY)] * 3,
        out_specs=[pl.BlockSpec(memory_space=pltpu.VMEM), pl.BlockSpec(memory_space=pl.ANY)],
        out_shape=[
            jax.ShapeDtypeStruct((GROUPS, all_pairs, PAIR_ROWS, SECTION), jnp.bfloat16),
            jax.ShapeDtypeStruct((2 * EARLY_PAIRS * FRAME_ROWS, SECTION), rows.dtype),
        ],
        scratch_shapes=[
            pltpu.VMEM(((2 * pairs + TAPS - 1) * FRAME_ROWS, SECTION), jnp.int32),
            pltpu.VMEM(tables.shape, tables.dtype),
            pltpu.VMEM(waves.shape, waves.dtype),
            pltpu.VMEM((3, GROUPS * PAIR_ROWS, SECTION), jnp.float32),
            pltpu.SemaphoreType.DMA((pairs,)),
            pltpu.SemaphoreType.DMA((2,)),
            pltpu.SemaphoreType.DMA,
        ],
        compiler_params=pltpu.CompilerParams(vmem_limit_bytes=LATE_VMEM_BYTES),
        cost_estimate=channelizer_cost(pairs),
        name="channelize_late",
    )(rows, *padded)


def early_kernel(history, rows, tables, waves, into, out, strided):
    rim = TAPS - 1

    def loader(pair):
        def load(t, i):
            frame = 2 * pair + t - rim
            if frame < 0:
                at = (frame + rim) * FRAME_ROWS + i
                return history[pl.ds(at, OUTER, stride=INPUTS_HERE), :] + ZERO_SAMPLE
            return rows[pl.ds(frame * FRAME_ROWS + i, OUTER, stride=INPUTS_HERE), :]

        return load

    def finish(pair, spectra):
        out[:, pair] = spectra

    channelize_pairs(
        [loader(pair) for pair in range(EARLY_PAIRS)], tables, waves, strided, finish
    )


def channelize_early(history, rows, tables, waves, into):
    near, far = pl.BlockSpec(memory_space=pltpu.VMEM), pl.BlockSpec(memory_space=pl.ANY)
    return pl.pallas_call(
        early_kernel,
        in_specs=[near, near, near, near, near],
        out_specs=near,
        out_shape=jax.ShapeDtypeStruct(into.shape, into.dtype),
        scratch_shapes=[
            pltpu.VMEM((EARLY_PAIRS, GROUPS * PAIR_ROWS, SECTION), jnp.float32),
        ],
        input_output_aliases={4: 0},
        compiler_params=pltpu.CompilerParams(vmem_limit_bytes=EARLY_VMEM_BYTES),
        cost_estimate=channelizer_cost(EARLY_PAIRS),
        name="channelize_early",
    )(history, rows, jnp.asarray(tables), jnp.asarray(waves), into)


def spread_tables():
    even = np.zeros((INPUTS, INPUTS, 2))
    odd = np.zeros((INPUTS, INPUTS, 2))
    inputs = np.arange(INPUTS).reshape(GROUPS, INPUTS_HERE)[ORDER].reshape(INPUTS)
    even[inputs, np.arange(INPUTS), 0] = 1.0
    odd[inputs, np.arange(INPUTS), 1] = 1.0
    even = even.reshape(INPUTS, 2 * INPUTS)
    odd = odd.reshape(INPUTS, 2 * INPUTS)
    upper = np.concatenate([even, -odd], axis=0)
    lower = np.concatenate([odd, even], axis=0)
    return upper.astype(jnp.bfloat16), lower.astype(jnp.bfloat16)


def weights_kernel(packed_ref, upper, lower, out):
    packed = packed_ref[...]
    parts = jnp.concatenate(
        [
            ((packed >> 6) - 32).astype(jnp.float32).astype(jnp.bfloat16),
            ((packed & 63) - 32).astype(jnp.float32).astype(jnp.bfloat16),
        ],
        axis=1,
    )
    out[:BEAMS] = jnp.dot(parts, upper[...], preferred_element_type=jnp.float32).astype(
        jnp.bfloat16
    )
    out[BEAMS:] = jnp.dot(parts, lower[...], preferred_element_type=jnp.float32).astype(
        jnp.bfloat16
    )


def stacked_weights(packed):
    upper, lower = spread_tables()
    return pl.pallas_call(
        weights_kernel,
        out_shape=jax.ShapeDtypeStruct((2 * BEAMS, 2 * INPUTS), jnp.bfloat16),
        in_specs=[pl.BlockSpec(memory_space=pltpu.VMEM)] * 3,
        out_specs=pl.BlockSpec(memory_space=pltpu.VMEM),
        compiler_params=pltpu.CompilerParams(vmem_limit_bytes=BEAM_VMEM_BYTES),
        cost_estimate=pl.CostEstimate(
            flops=2 * 2 * BEAMS * 512 * 512, bytes_accessed=5 * 2**20, transcendentals=0
        ),
        name="stack_weights",
    )(packed, jnp.asarray(upper), jnp.asarray(lower))


BEAM_BLOCK = 256


def beams_kernel(weights_ref, spectra_ref, out, total):
    pairs = range(spectra_ref.shape[1])
    blocks = range(0, BEAMS, BEAM_BLOCK)

    def paired(pair):
        spectra = spectra_ref[:, pair].astype(jnp.float32)
        return jnp.concatenate(
            [
                spectra[:, half * 8 : half * 8 + 8].reshape(2 * INPUTS, SECTION).astype(jnp.bfloat16)
                for half in range(2)
            ],
            axis=1,
        )

    def formed(at, values):
        return jnp.dot(
            weights_ref[at : at + BEAM_BLOCK], values, preferred_element_type=jnp.float32
        )

    values = {}
    for block, at in enumerate(blocks):
        for pair in pairs:
            if block == 0:
                values[pair] = paired(pair)
            real_part = formed(at, values[pair])
            imag_part = formed(BEAMS + at, values[pair])
            powers = real_part * real_part + imag_part * imag_part
            total[at : at + BEAM_BLOCK] = (
                powers if pair == 0 else total[at : at + BEAM_BLOCK] + powers
            )
    scale = 1.0 / (24.0 * math.sqrt(INPUTS)) ** 2 / AVERAGE
    lane = lax.broadcasted_iota(jnp.int32, (BEAMS, SECTION), 1)
    sums = []
    for half in range(2):
        part = total[:, half * SECTION : (half + 1) * SECTION]
        sums.append((part + pltpu.roll(part, OUTER, 1)) * scale)
    out[...] = jnp.where(lane < OUTER, sums[0], sums[1])


def beams(weights, spectra):
    pairs = spectra.shape[1]
    return pl.pallas_call(
        beams_kernel,
        in_specs=[pl.BlockSpec(memory_space=pltpu.VMEM)] * 2,
        out_specs=pl.BlockSpec(memory_space=pltpu.VMEM),
        out_shape=jax.ShapeDtypeStruct((BEAMS, SECTION), jnp.float32),
        scratch_shapes=[pltpu.VMEM((BEAMS, 2 * SECTION), jnp.float32)],
        compiler_params=pltpu.CompilerParams(vmem_limit_bytes=BEAM_VMEM_BYTES),
        cost_estimate=pl.CostEstimate(
            flops=pairs * 2 * 1536 * 512 * 256,
            bytes_accessed=1536 * 512 * 2 + pairs * 262144 + 768 * 128 * 4,
            transcendentals=0,
        ),
        name="beams",
    )(weights, spectra)


def per_device(voltages, beam_weights):
    inputs_here, own_len = voltages.shape
    pairs = own_len // CHANNELS // 2
    rows = jnp.transpose(voltages.reshape(inputs_here, own_len // SECTION, SECTION), (1, 0, 2))
    rows = rows.reshape(own_len // SECTION * inputs_here, SECTION)
    rim = (TAPS - 1) * FRAME_ROWS
    devices = lax.axis_size("tm")
    history = lax.ppermute(
        rows[rows.shape[0] - rim :] - ZERO_SAMPLE,
        "tm",
        [(i, i + 1) for i in range(devices - 1)],
    )
    tables, waves = channelizer_tables()
    spectra, head = channelize_late(rows, tables, waves, pairs)
    spectra, packed_weights = lax.optimization_barrier((spectra, beam_weights[0]))
    weights = stacked_weights(packed_weights)
    spectra = channelize_early(history, head, tables, waves, spectra)
    spectra, weights = lax.optimization_barrier((spectra, weights))
    turned = lax.all_to_all(spectra, "chan", 0, 0, axis_index_groups=[ORDER], tiled=True)
    averaged = beams(weights, turned)
    return lax.all_to_all(averaged[None], "chan", split_axis=1, concat_axis=2, tiled=True)


def solution(mesh):
    return jax.shard_map(
        per_device,
        mesh=mesh,
        in_specs=(P("chan", "tm"), P("chan", None, None)),
        out_specs=P("tm", "chan", None),
        check_vma=False,
    )
```

```python
import functools
import math

import jax
import jax.numpy as jnp
import numpy as np
from jax import lax
from jax.experimental import pallas as pl
from jax.experimental.pallas import tpu as pltpu
from jax.sharding import PartitionSpec as P

INPUTS = 256
BEAMS = 768
CHANNELS = 8192
SECTION = 128
TAPS = 4
AVERAGE = 16
OUTER = 64
GROUPS = 64
ZERO_SAMPLE = 32 * 64 + 32
TABLE_ROOM = 6144
LATE_VMEM_BYTES = 51 * 1024 * 1024
EARLY_VMEM_BYTES = 50 * 1024 * 1024
BEAM_VMEM_BYTES = 32 * 1024 * 1024

INPUTS_HERE = 4
FRAME_ROWS = OUTER * INPUTS_HERE
PAIR_ROWS = 16
EARLY_PAIRS = 2
BEAMS_HERE = BEAMS // GROUPS
ORDER = [
    4, 47, 59, 35, 43, 22, 6, 18, 60, 56, 24, 20, 44, 34, 63, 10,
    7, 54, 5, 57, 33, 19, 8, 48, 13, 27, 17, 45, 62, 26, 55, 40,
    16, 2, 37, 41, 11, 14, 46, 25, 32, 36, 21, 23, 30, 29, 53, 38,
    3, 1, 51, 50, 61, 0, 52, 28, 49, 31, 15, 39, 9, 42, 12, 58,
]


def split_table(table):
    high = table.astype(jnp.bfloat16)
    low = (table - np.asarray(high, np.float64)).astype(jnp.bfloat16)
    return np.asarray(high), np.asarray(low)


def pfb_taper():
    places = np.arange(TAPS * CHANNELS, dtype=np.float64)
    length = TAPS * CHANNELS
    offsets = (places - 0.5 * length + 0.5) / CHANNELS
    hann_window = 0.5 - 0.5 * np.cos(2.0 * math.pi * (places + 0.5) / length)
    taper = np.sinc(offsets) * hann_window
    return taper.astype(np.float32).reshape(TAPS, OUTER, SECTION)


def phasors(left_index, right_index, length):
    turns = np.outer(left_index, right_index) % length
    angles = turns * (-2.0 * math.pi / length)
    return np.cos(angles), np.sin(angles)


def outer_table():
    cos_part, sin_part = phasors(np.arange(OUTER), np.arange(OUTER), OUTER)
    table = np.zeros((2, 2, OUTER, 2, 2, OUTER))
    for f in range(2):
        table[0, f, :, f, 0, :] = cos_part
        table[0, f, :, f, 1, :] = -sin_part
        table[1, f, :, f, 0, :] = sin_part
        table[1, f, :, f, 1, :] = cos_part
    return table.reshape(4 * OUTER, 4 * OUTER)


def twist_table():
    norm = 1.0 / (32.0 * math.sqrt(CHANNELS))
    cos_part, sin_part = phasors(np.arange(OUTER), np.arange(SECTION), CHANNELS)
    return (
        np.tile(cos_part * norm, (2, 1)).astype(np.float32),
        np.tile(sin_part * norm, (2, 1)).astype(np.float32),
    )


def inner_table():
    channel = np.arange(SECTION).reshape(GROUPS, 2)[ORDER].T
    table = np.zeros((2, 2, GROUPS, 2, SECTION))
    for half in range(2):
        cos_part, sin_part = phasors(channel[half], np.arange(SECTION), SECTION)
        table[half, 0, :, 0, :] = cos_part
        table[half, 0, :, 1, :] = -sin_part
        table[half, 1, :, 0, :] = sin_part
        table[half, 1, :, 1, :] = cos_part
    return table.reshape(4 * GROUPS, 2 * SECTION)


def two_halves(values):
    high = values.astype(jnp.bfloat16)
    low = (values - high.astype(jnp.float32)).astype(jnp.bfloat16)
    return high, low


def careful_dot(left_high, left_low, right, contract):
    right_high, right_low = two_halves(right)
    dims = (contract, ((), ()))

    def dot(left, values):
        return lax.dot_general(left, values, dims, preferred_element_type=jnp.float32)

    return dot(left_high, right_high) + (dot(left_high, right_low) + dot(left_low, right_high))


def filtered(load, waves, inputs):
    columns = []
    for i in inputs:
        summed = {}
        for t in range(TAPS + 1):
            packed = load(t, i)
            parts = (
                ((packed >> 6) - 32).astype(jnp.float32),
                ((packed & 63) - 32).astype(jnp.float32),
            )
            for f in range(2):
                if 0 <= t - f < TAPS:
                    tap = waves[(t - f) * OUTER : (t - f + 1) * OUTER]
                    for part in range(2):
                        term = parts[part] * tap
                        key = (f, part)
                        summed[key] = summed[key] + term if key in summed else term
        columns.append(
            jnp.concatenate([summed[f, part] for f in range(2) for part in range(2)], axis=0)
        )
    return jnp.concatenate(columns, axis=1)


def twisted(first, waves, count):
    cos_part = waves[TAPS * OUTER : TAPS * OUTER + SECTION]
    sin_part = waves[TAPS * OUTER + SECTION : TAPS * OUTER + 2 * SECTION]
    turned = []
    for i in range(count):
        real_part = first[:SECTION, i * SECTION : (i + 1) * SECTION]
        imag_part = first[SECTION:, i * SECTION : (i + 1) * SECTION]
        turned.append(
            jnp.concatenate(
                [
                    real_part * cos_part - imag_part * sin_part,
                    real_part * sin_part + imag_part * cos_part,
                ],
                axis=1,
            )
        )
    return jnp.concatenate(turned, axis=0)


def interleave(spectra, inputs, strided):
    for half in range(2):
        for part in range(2):
            top = (half * 2 + part) * GROUPS
            for at, i in enumerate(inputs):
                row = half * 8 + i * 2 + part
                strided[pl.ds(row, GROUPS, stride=PAIR_ROWS), :] = spectra[
                    top : top + GROUPS, at * SECTION : (at + 1) * SECTION
                ]


def channelize_pairs(loads, tables, waves, strided, finish):
    size = 4 * OUTER
    sets = [(0, 1), (2, 3)]
    steps = [(pair, inputs) for pair in range(len(loads)) for inputs in sets]
    frames = filtered(loads[0], waves, sets[0])
    for number, (pair, inputs) in enumerate(steps):
        first = careful_dot(tables[:size], tables[size : 2 * size], frames, ((1,), (0,)))
        if number + 1 < len(steps):
            next_pair, next_inputs = steps[number + 1]
            frames = filtered(loads[next_pair], waves, next_inputs)
        turned = twisted(first, waves, len(inputs))
        spectra = careful_dot(
            tables[2 * size : 3 * size], tables[3 * size : 4 * size], turned, ((1,), (1,))
        )
        interleave(spectra, inputs, strided.at[pair])
        if inputs == sets[-1]:
            finish(pair, strided[pair].astype(jnp.bfloat16).reshape(GROUPS, PAIR_ROWS, SECTION))


def late_kernel(
    rows, tables_in, waves_in, out, head,
    frames, tables, waves, strided, frame_sem, table_sem, head_sem,
):
    pairs = frame_sem.shape[0]
    start = (2 * EARLY_PAIRS - (TAPS - 1)) * FRAME_ROWS
    step = 2 * FRAME_ROWS
    lead = (TAPS - 1) * FRAME_ROWS

    def fetch(pair):
        at = 0 if isinstance(pair, int) else lead + pair * step
        size = lead + step if isinstance(pair, int) else step
        return pltpu.make_async_copy(
            rows.at[pl.ds(start + at, size)], frames.at[pl.ds(at, size)], frame_sem.at[pair]
        )

    table_copies = [
        pltpu.make_async_copy(waves_in.at[pl.ds(0, waves.shape[0])], waves, table_sem.at[0]),
        pltpu.make_async_copy(tables_in.at[pl.ds(0, tables.shape[0])], tables, table_sem.at[1]),
    ]
    table_copies[0].start()
    fetch(0).start()
    table_copies[1].start()

    @pl.loop(1, pairs)
    def _(pair):
        fetch(pair).start()

    head_copy = pltpu.make_async_copy(rows.at[pl.ds(0, head.shape[0])], head, head_sem)
    head_copy.start()
    for copy in table_copies:
        copy.wait()
    fetch(0).wait()

    @pl.loop(1, pairs)
    def _(pair):
        fetch(pair).wait()

    def loader(pair):
        def load(t, i):
            at = pair * step + t * FRAME_ROWS + i
            return frames[pl.ds(at, OUTER, stride=INPUTS_HERE), :]

        return load

    @pl.loop(0, pairs // 3)
    def _(turn):
        def finish(pair, spectra):
            out[:, EARLY_PAIRS + turn * 3 + pair] = spectra

        loads = [loader(turn * 3 + pair) for pair in range(3)]
        channelize_pairs(loads, tables, waves, strided, finish)

    head_copy.wait()


def channelizer_tables():
    outer_high, outer_low = split_table(outer_table())
    inner_high, inner_low = split_table(inner_table())
    twist_cos, twist_sin = twist_table()
    tables = np.concatenate([outer_high, outer_low, inner_high, inner_low], axis=0)
    taper = pfb_taper().reshape(TAPS * OUTER, SECTION)
    waves = np.concatenate([taper, twist_cos, twist_sin], axis=0)
    return tables, waves


def channelizer_cost(pairs):
    return pl.CostEstimate(
        flops=pairs * 3 * 2 * 2 * 256 * 256 * 512,
        bytes_accessed=pairs * 2 * 262144 + 2**20,
        transcendentals=0,
    )


def channelize_late(rows, tables, waves, all_pairs):
    pairs = all_pairs - EARLY_PAIRS
    padded = [
        jnp.asarray(np.pad(table, ((0, TABLE_ROOM - table.shape[0]), (0, 0))))
        for table in (tables, waves)
    ]
    return pl.pallas_call(
        late_kernel,
        in_specs=[pl.BlockSpec(memory_space=pl.ANY)] * 3,
        out_specs=[pl.BlockSpec(memory_space=pltpu.VMEM), pl.BlockSpec(memory_space=pl.ANY)],
        out_shape=[
            jax.ShapeDtypeStruct((GROUPS, all_pairs, PAIR_ROWS, SECTION), jnp.bfloat16),
            jax.ShapeDtypeStruct((2 * EARLY_PAIRS * FRAME_ROWS, SECTION), rows.dtype),
        ],
        scratch_shapes=[
            pltpu.VMEM(((2 * pairs + TAPS - 1) * FRAME_ROWS, SECTION), jnp.int32),
            pltpu.VMEM(tables.shape, tables.dtype),
            pltpu.VMEM(waves.shape, waves.dtype),
            pltpu.VMEM((3, GROUPS * PAIR_ROWS, SECTION), jnp.float32),
            pltpu.SemaphoreType.DMA((pairs,)),
            pltpu.SemaphoreType.DMA((2,)),
            pltpu.SemaphoreType.DMA,
        ],
        compiler_params=pltpu.CompilerParams(vmem_limit_bytes=LATE_VMEM_BYTES),
        cost_estimate=channelizer_cost(pairs),
        name="channelize_late",
    )(rows, *padded)


def early_kernel(history, rows, tables, waves, into, out, strided):
    rim = TAPS - 1

    def loader(pair):
        def load(t, i):
            frame = 2 * pair + t - rim
            if frame < 0:
                at = (frame + rim) * FRAME_ROWS + i
                return history[pl.ds(at, OUTER, stride=INPUTS_HERE), :] + ZERO_SAMPLE
            return rows[pl.ds(frame * FRAME_ROWS + i, OUTER, stride=INPUTS_HERE), :]

        return load

    def finish(pair, spectra):
        out[:, pair] = spectra

    channelize_pairs(
        [loader(pair) for pair in range(EARLY_PAIRS)], tables, waves, strided, finish
    )


def channelize_early(history, rows, tables, waves, into):
    near, far = pl.BlockSpec(memory_space=pltpu.VMEM), pl.BlockSpec(memory_space=pl.ANY)
    return pl.pallas_call(
        early_kernel,
        in_specs=[near, near, near, near, near],
        out_specs=near,
        out_shape=jax.ShapeDtypeStruct(into.shape, into.dtype),
        scratch_shapes=[
            pltpu.VMEM((EARLY_PAIRS, GROUPS * PAIR_ROWS, SECTION), jnp.float32),
        ],
        input_output_aliases={4: 0},
        compiler_params=pltpu.CompilerParams(vmem_limit_bytes=EARLY_VMEM_BYTES),
        cost_estimate=channelizer_cost(EARLY_PAIRS),
        name="channelize_early",
    )(history, rows, jnp.asarray(tables), jnp.asarray(waves), into)


def spread_tables():
    even = np.zeros((INPUTS, INPUTS, 2))
    odd = np.zeros((INPUTS, INPUTS, 2))
    inputs = np.arange(INPUTS).reshape(GROUPS, INPUTS_HERE)[ORDER].reshape(INPUTS)
    even[inputs, np.arange(INPUTS), 0] = 1.0
    odd[inputs, np.arange(INPUTS), 1] = 1.0
    even = even.reshape(INPUTS, 2 * INPUTS)
    odd = odd.reshape(INPUTS, 2 * INPUTS)
    upper = np.concatenate([even, -odd], axis=0)
    lower = np.concatenate([odd, even], axis=0)
    return upper.astype(jnp.bfloat16), lower.astype(jnp.bfloat16)


def weights_kernel(packed_ref, upper, lower, out, ordered):
    for p, device in enumerate(ORDER):
        ordered[pl.ds(BEAMS_HERE * p, BEAMS_HERE), :] = packed_ref[
            pl.ds(BEAMS_HERE * device, BEAMS_HERE), :
        ]
    packed = ordered[...]
    parts = jnp.concatenate(
        [
            ((packed >> 6) - 32).astype(jnp.float32).astype(jnp.bfloat16),
            ((packed & 63) - 32).astype(jnp.float32).astype(jnp.bfloat16),
        ],
        axis=1,
    )
    out[:BEAMS] = jnp.dot(parts, upper[...], preferred_element_type=jnp.float32).astype(
        jnp.bfloat16
    )
    out[BEAMS:] = jnp.dot(parts, lower[...], preferred_element_type=jnp.float32).astype(
        jnp.bfloat16
    )


def stacked_weights(packed):
    upper, lower = spread_tables()
    return pl.pallas_call(
        weights_kernel,
        out_shape=jax.ShapeDtypeStruct((2 * BEAMS, 2 * INPUTS), jnp.bfloat16),
        in_specs=[pl.BlockSpec(memory_space=pltpu.VMEM)] * 3,
        out_specs=pl.BlockSpec(memory_space=pltpu.VMEM),
        scratch_shapes=[pltpu.VMEM((BEAMS, INPUTS), jnp.int32)],
        compiler_params=pltpu.CompilerParams(vmem_limit_bytes=BEAM_VMEM_BYTES),
        cost_estimate=pl.CostEstimate(
            flops=2 * 2 * BEAMS * 512 * 512, bytes_accessed=5 * 2**20, transcendentals=0
        ),
        name="stack_weights",
    )(packed, jnp.asarray(upper), jnp.asarray(lower))


BEAM_BLOCK = 256
CODED_ROWS = 16
SMALLEST_POWER = 2.0**-120


def beams_kernel(weights_ref, spectra_ref, out, total, averaged, coded):
    pairs = range(spectra_ref.shape[1])
    blocks = range(0, BEAMS, BEAM_BLOCK)

    def paired(pair):
        spectra = spectra_ref[:, pair].astype(jnp.float32)
        return jnp.concatenate(
            [
                spectra[:, half * 8 : half * 8 + 8].reshape(2 * INPUTS, SECTION).astype(jnp.bfloat16)
                for half in range(2)
            ],
            axis=1,
        )

    def formed(at, values):
        return jnp.dot(
            weights_ref[at : at + BEAM_BLOCK], values, preferred_element_type=jnp.float32
        )

    values = {}
    for block, at in enumerate(blocks):
        for pair in pairs:
            if block == 0:
                values[pair] = paired(pair)
            real_part = formed(at, values[pair])
            imag_part = formed(BEAMS + at, values[pair])
            powers = real_part * real_part + imag_part * imag_part
            total[at : at + BEAM_BLOCK] = (
                powers if pair == 0 else total[at : at + BEAM_BLOCK] + powers
            )
    scale = 1.0 / (24.0 * math.sqrt(INPUTS)) ** 2 / AVERAGE
    lane = lax.broadcasted_iota(jnp.int32, (BEAMS, SECTION), 1)
    sums = []
    for half in range(2):
        part = total[:, half * SECTION : (half + 1) * SECTION]
        sums.append((part + pltpu.roll(part, OUTER, 1)) * scale)
    averaged[...] = jnp.where(lane < OUTER, sums[0], sums[1])
    lane = lax.broadcasted_iota(jnp.int32, (GROUPS, SECTION), 1)
    exponents = jnp.zeros((GROUPS, SECTION), jnp.float32)
    coded[...] = jnp.zeros_like(coded)
    for beam in range(BEAMS_HERE):
        power = averaged[pl.ds(beam, GROUPS, stride=BEAMS_HERE), :]
        top = jnp.maximum(jnp.max(power, axis=1, keepdims=True), SMALLEST_POWER)
        exponent = jnp.floor(jnp.log2(top)) + 1.0
        steps = jnp.floor(power * jnp.exp2(-exponent) * 32768.0 + 0.5)
        coded[pl.ds(beam, GROUPS, stride=CODED_ROWS), :] = jnp.minimum(steps, 32767.0)
        exponents = jnp.where(lane == beam, exponent, exponents)
    coded[pl.ds(BEAMS_HERE, GROUPS, stride=CODED_ROWS), :] = exponents
    out[...] = coded[...].astype(jnp.int32).astype(jnp.int16).reshape(out.shape)


def beams(weights, spectra):
    pairs = spectra.shape[1]
    return pl.pallas_call(
        beams_kernel,
        in_specs=[pl.BlockSpec(memory_space=pltpu.VMEM)] * 2,
        out_specs=pl.BlockSpec(memory_space=pltpu.VMEM),
        out_shape=jax.ShapeDtypeStruct((GROUPS, CODED_ROWS, SECTION), jnp.int16),
        scratch_shapes=[
            pltpu.VMEM((BEAMS, 2 * SECTION), jnp.float32),
            pltpu.VMEM((BEAMS, SECTION), jnp.float32),
            pltpu.VMEM((GROUPS * CODED_ROWS, SECTION), jnp.float32),
        ],
        compiler_params=pltpu.CompilerParams(vmem_limit_bytes=BEAM_VMEM_BYTES),
        cost_estimate=pl.CostEstimate(
            flops=pairs * 2 * 1536 * 512 * 256,
            bytes_accessed=1536 * 512 * 2 + pairs * 262144 + 768 * 128 * 4,
            transcendentals=0,
        ),
        name="beams",
    )(weights, spectra)


def decode_kernel(coded_ref, out, values):
    values[...] = coded_ref[...].astype(jnp.int32).astype(jnp.float32).reshape(values.shape)
    exponents = values[pl.ds(BEAMS_HERE, GROUPS, stride=CODED_ROWS), :]
    for beam in range(BEAMS_HERE):
        scale = jnp.exp2(exponents[:, beam : beam + 1]) * 2.0**-15
        rows = pl.ds(beam, GROUPS, stride=CODED_ROWS)
        values[rows, :] = values[rows, :] * scale
    for p, device in enumerate(ORDER):
        out[pl.ds(device, BEAMS_HERE, stride=GROUPS), :] = values[
            pl.ds(CODED_ROWS * p, BEAMS_HERE), :
        ]


def decode(coded):
    return pl.pallas_call(
        decode_kernel,
        in_specs=[pl.BlockSpec(memory_space=pltpu.VMEM)],
        out_specs=pl.BlockSpec(memory_space=pltpu.VMEM),
        out_shape=jax.ShapeDtypeStruct((BEAMS_HERE * GROUPS, SECTION), jnp.float32),
        scratch_shapes=[pltpu.VMEM((GROUPS * CODED_ROWS, SECTION), jnp.float32)],
        compiler_params=pltpu.CompilerParams(vmem_limit_bytes=BEAM_VMEM_BYTES),
        name="decode",
    )(coded)


def per_device(voltages, beam_weights):
    inputs_here, own_len = voltages.shape
    pairs = own_len // CHANNELS // 2
    rows = jnp.transpose(voltages.reshape(inputs_here, own_len // SECTION, SECTION), (1, 0, 2))
    rows = rows.reshape(own_len // SECTION * inputs_here, SECTION)
    rim = (TAPS - 1) * FRAME_ROWS
    devices = lax.axis_size("tm")
    history = lax.ppermute(
        rows[rows.shape[0] - rim :] - ZERO_SAMPLE,
        "tm",
        [(i, i + 1) for i in range(devices - 1)],
    )
    tables, waves = channelizer_tables()
    spectra, head = channelize_late(rows, tables, waves, pairs)
    spectra, packed_weights = lax.optimization_barrier((spectra, beam_weights[0]))
    weights = stacked_weights(packed_weights)
    spectra = channelize_early(history, head, tables, waves, spectra)
    spectra, weights = lax.optimization_barrier((spectra, weights))
    turned = lax.all_to_all(spectra, "chan", 0, 0, axis_index_groups=[ORDER], tiled=True)
    coded = beams(weights, turned)
    received = lax.all_to_all(coded, "chan", 0, 0, axis_index_groups=[ORDER], tiled=True)
    return decode(received).reshape(1, BEAMS_HERE, CHANNELS)


def solution(mesh):
    return jax.shard_map(
        per_device,
        mesh=mesh,
        in_specs=(P("chan", "tm"), P("chan", None, None)),
        out_specs=P("tm", "chan", None),
        check_vma=False,
    )
```

```python
import functools
import math

import jax
import jax.numpy as jnp
import numpy as np
from jax import lax
from jax.experimental import pallas as pl
from jax.experimental.pallas import tpu as pltpu
from jax.sharding import PartitionSpec as P

INPUTS = 256
BEAMS = 768
CHANNELS = 8192
SECTION = 128
TAPS = 4
AVERAGE = 16
OUTER = 64
GROUPS = 64
ZERO_SAMPLE = 32 * 64 + 32
TABLE_ROOM = 6144
LATE_VMEM_BYTES = 51 * 1024 * 1024
EARLY_VMEM_BYTES = 50 * 1024 * 1024
BEAM_VMEM_BYTES = 32 * 1024 * 1024

INPUTS_HERE = 4
FRAME_ROWS = OUTER * INPUTS_HERE
PAIR_ROWS = 16
EARLY_PAIRS = 2
BEAMS_HERE = BEAMS // GROUPS
STRIDE_ROOM = 16
ORDER = [
    4, 47, 59, 35, 43, 22, 6, 18, 60, 56, 24, 20, 44, 34, 63, 10,
    7, 54, 5, 57, 33, 19, 8, 48, 13, 27, 17, 45, 62, 26, 55, 40,
    16, 2, 37, 41, 11, 14, 46, 25, 32, 36, 21, 23, 30, 29, 53, 38,
    3, 1, 51, 50, 61, 0, 52, 28, 49, 31, 15, 39, 9, 42, 12, 58,
]


def split_table(table):
    high = table.astype(jnp.bfloat16)
    low = (table - np.asarray(high, np.float64)).astype(jnp.bfloat16)
    return np.asarray(high), np.asarray(low)


def pfb_taper():
    places = np.arange(TAPS * CHANNELS, dtype=np.float64)
    length = TAPS * CHANNELS
    offsets = (places - 0.5 * length + 0.5) / CHANNELS
    hann_window = 0.5 - 0.5 * np.cos(2.0 * math.pi * (places + 0.5) / length)
    taper = np.sinc(offsets) * hann_window
    return taper.astype(np.float32).reshape(TAPS, OUTER, SECTION)


def phasors(left_index, right_index, length):
    turns = np.outer(left_index, right_index) % length
    angles = turns * (-2.0 * math.pi / length)
    return np.cos(angles), np.sin(angles)


def outer_table():
    cos_part, sin_part = phasors(np.arange(OUTER), np.arange(OUTER), OUTER)
    table = np.zeros((2, 2, OUTER, 2, 2, OUTER))
    for f in range(2):
        table[0, f, :, f, 0, :] = cos_part
        table[0, f, :, f, 1, :] = -sin_part
        table[1, f, :, f, 0, :] = sin_part
        table[1, f, :, f, 1, :] = cos_part
    return table.reshape(4 * OUTER, 4 * OUTER)


def twist_table():
    norm = 1.0 / (32.0 * math.sqrt(CHANNELS))
    cos_part, sin_part = phasors(np.arange(OUTER), np.arange(SECTION), CHANNELS)
    return (
        np.tile(cos_part * norm, (2, 1)).astype(np.float32),
        np.tile(sin_part * norm, (2, 1)).astype(np.float32),
    )


def inner_table():
    channel = np.arange(SECTION).reshape(GROUPS, 2)[ORDER].T
    table = np.zeros((2, 2, GROUPS, 2, SECTION))
    for half in range(2):
        cos_part, sin_part = phasors(channel[half], np.arange(SECTION), SECTION)
        table[half, 0, :, 0, :] = cos_part
        table[half, 0, :, 1, :] = -sin_part
        table[half, 1, :, 0, :] = sin_part
        table[half, 1, :, 1, :] = cos_part
    return table.reshape(4 * GROUPS, 2 * SECTION)


def two_halves(values):
    high = values.astype(jnp.bfloat16)
    low = (values - high.astype(jnp.float32)).astype(jnp.bfloat16)
    return high, low


def careful_dot(left_high, left_low, right, contract):
    right_high, right_low = two_halves(right)
    dims = (contract, ((), ()))

    def dot(left, values):
        return lax.dot_general(left, values, dims, preferred_element_type=jnp.float32)

    return dot(left_high, right_high) + (dot(left_high, right_low) + dot(left_low, right_high))


def filtered(load, waves, inputs):
    columns = []
    for i in inputs:
        summed = {}
        for t in range(TAPS + 1):
            packed = load(t, i)
            parts = (
                ((packed >> 6) - 32).astype(jnp.float32),
                ((packed & 63) - 32).astype(jnp.float32),
            )
            for f in range(2):
                if 0 <= t - f < TAPS:
                    tap = waves[(t - f) * OUTER : (t - f + 1) * OUTER]
                    for part in range(2):
                        term = parts[part] * tap
                        key = (f, part)
                        summed[key] = summed[key] + term if key in summed else term
        columns.append(
            jnp.concatenate([summed[f, part] for f in range(2) for part in range(2)], axis=0)
        )
    return jnp.concatenate(columns, axis=1)


def twisted(first, waves, count):
    cos_part = waves[TAPS * OUTER : TAPS * OUTER + SECTION]
    sin_part = waves[TAPS * OUTER + SECTION : TAPS * OUTER + 2 * SECTION]
    turned = []
    for i in range(count):
        real_part = first[:SECTION, i * SECTION : (i + 1) * SECTION]
        imag_part = first[SECTION:, i * SECTION : (i + 1) * SECTION]
        turned.append(
            jnp.concatenate(
                [
                    real_part * cos_part - imag_part * sin_part,
                    real_part * sin_part + imag_part * cos_part,
                ],
                axis=1,
            )
        )
    return jnp.concatenate(turned, axis=0)


def interleave(spectra, inputs, strided):
    for half in range(2):
        for part in range(2):
            top = (half * 2 + part) * GROUPS
            for at, i in enumerate(inputs):
                row = half * 8 + i * 2 + part
                strided[pl.ds(row, GROUPS, stride=PAIR_ROWS), :] = spectra[
                    top : top + GROUPS, at * SECTION : (at + 1) * SECTION
                ]


def channelize_pairs(loads, tables, waves, strided, finish):
    size = 4 * OUTER
    sets = [(0, 1), (2, 3)]
    steps = [(pair, inputs) for pair in range(len(loads)) for inputs in sets]
    frames = filtered(loads[0], waves, sets[0])
    for number, (pair, inputs) in enumerate(steps):
        first = careful_dot(tables[:size], tables[size : 2 * size], frames, ((1,), (0,)))
        if number + 1 < len(steps):
            next_pair, next_inputs = steps[number + 1]
            frames = filtered(loads[next_pair], waves, next_inputs)
        turned = twisted(first, waves, len(inputs))
        spectra = careful_dot(
            tables[2 * size : 3 * size], tables[3 * size : 4 * size], turned, ((1,), (1,))
        )
        interleave(spectra, inputs, strided.at[pair])
        if inputs == sets[-1]:
            rows = strided[pair, : GROUPS * PAIR_ROWS].astype(jnp.bfloat16)
            finish(pair, rows.reshape(GROUPS, PAIR_ROWS, SECTION))


def late_kernel(
    rows, tables_in, waves_in, out, head,
    frames, tables, waves, strided, frame_sem, table_sem, head_sem,
):
    pairs = frame_sem.shape[0]
    start = (2 * EARLY_PAIRS - (TAPS - 1)) * FRAME_ROWS
    step = 2 * FRAME_ROWS
    lead = (TAPS - 1) * FRAME_ROWS

    def fetch(pair):
        at = 0 if isinstance(pair, int) else lead + pair * step
        size = lead + step if isinstance(pair, int) else step
        return pltpu.make_async_copy(
            rows.at[pl.ds(start + at, size)], frames.at[pl.ds(at, size)], frame_sem.at[pair]
        )

    table_copies = [
        pltpu.make_async_copy(waves_in.at[pl.ds(0, waves.shape[0])], waves, table_sem.at[0]),
        pltpu.make_async_copy(tables_in.at[pl.ds(0, tables.shape[0])], tables, table_sem.at[1]),
    ]
    table_copies[0].start()
    fetch(0).start()
    table_copies[1].start()

    @pl.loop(1, pairs)
    def _(pair):
        fetch(pair).start()

    head_copy = pltpu.make_async_copy(rows.at[pl.ds(0, head.shape[0])], head, head_sem)
    head_copy.start()
    for copy in table_copies:
        copy.wait()
    fetch(0).wait()

    @pl.loop(1, pairs)
    def _(pair):
        fetch(pair).wait()

    def loader(pair):
        def load(t, i):
            at = pair * step + t * FRAME_ROWS + i
            return frames[pl.ds(at, OUTER, stride=INPUTS_HERE), :]

        return load

    @pl.loop(0, pairs // 3)
    def _(turn):
        def finish(pair, spectra):
            out[:, EARLY_PAIRS + turn * 3 + pair] = spectra

        loads = [loader(turn * 3 + pair) for pair in range(3)]
        channelize_pairs(loads, tables, waves, strided, finish)

    head_copy.wait()


def channelizer_tables():
    outer_high, outer_low = split_table(outer_table())
    inner_high, inner_low = split_table(inner_table())
    twist_cos, twist_sin = twist_table()
    tables = np.concatenate([outer_high, outer_low, inner_high, inner_low], axis=0)
    taper = pfb_taper().reshape(TAPS * OUTER, SECTION)
    waves = np.concatenate([taper, twist_cos, twist_sin], axis=0)
    return tables, waves


def channelizer_cost(pairs):
    return pl.CostEstimate(
        flops=pairs * 3 * 2 * 2 * 256 * 256 * 512,
        bytes_accessed=pairs * 2 * 262144 + 2**20,
        transcendentals=0,
    )


def channelize_late(rows, tables, waves, all_pairs):
    pairs = all_pairs - EARLY_PAIRS
    padded = [
        jnp.asarray(np.pad(table, ((0, TABLE_ROOM - table.shape[0]), (0, 0))))
        for table in (tables, waves)
    ]
    return pl.pallas_call(
        late_kernel,
        in_specs=[pl.BlockSpec(memory_space=pl.ANY)] * 3,
        out_specs=[pl.BlockSpec(memory_space=pltpu.VMEM), pl.BlockSpec(memory_space=pl.ANY)],
        out_shape=[
            jax.ShapeDtypeStruct((GROUPS, all_pairs, PAIR_ROWS, SECTION), jnp.bfloat16),
            jax.ShapeDtypeStruct((2 * EARLY_PAIRS * FRAME_ROWS, SECTION), rows.dtype),
        ],
        scratch_shapes=[
            pltpu.VMEM(((2 * pairs + TAPS - 1) * FRAME_ROWS + STRIDE_ROOM, SECTION), jnp.int32),
            pltpu.VMEM(tables.shape, tables.dtype),
            pltpu.VMEM(waves.shape, waves.dtype),
            pltpu.VMEM((3, GROUPS * PAIR_ROWS + STRIDE_ROOM, SECTION), jnp.float32),
            pltpu.SemaphoreType.DMA((pairs,)),
            pltpu.SemaphoreType.DMA((2,)),
            pltpu.SemaphoreType.DMA,
        ],
        compiler_params=pltpu.CompilerParams(vmem_limit_bytes=LATE_VMEM_BYTES),
        cost_estimate=channelizer_cost(pairs),
        name="channelize_late",
    )(rows, *padded)


def early_kernel(history, rows, tables, waves, into, out, strided):
    rim = TAPS - 1

    def loader(pair):
        def load(t, i):
            frame = 2 * pair + t - rim
            if frame < 0:
                at = (frame + rim) * FRAME_ROWS + i
                return history[pl.ds(at, OUTER, stride=INPUTS_HERE), :] + ZERO_SAMPLE
            return rows[pl.ds(frame * FRAME_ROWS + i, OUTER, stride=INPUTS_HERE), :]

        return load

    def finish(pair, spectra):
        out[:, pair] = spectra

    out[:, EARLY_PAIRS:] = into[:, EARLY_PAIRS:]
    channelize_pairs(
        [loader(pair) for pair in range(EARLY_PAIRS)], tables, waves, strided, finish
    )


def channelize_early(history, rows, tables, waves, into):
    near, far = pl.BlockSpec(memory_space=pltpu.VMEM), pl.BlockSpec(memory_space=pl.ANY)
    return pl.pallas_call(
        early_kernel,
        in_specs=[near, near, near, near, near],
        out_specs=near,
        out_shape=jax.ShapeDtypeStruct(into.shape, into.dtype),
        scratch_shapes=[
            pltpu.VMEM((EARLY_PAIRS, GROUPS * PAIR_ROWS + STRIDE_ROOM, SECTION), jnp.float32),
        ],
        input_output_aliases={4: 0},
        compiler_params=pltpu.CompilerParams(vmem_limit_bytes=EARLY_VMEM_BYTES),
        cost_estimate=channelizer_cost(EARLY_PAIRS),
        name="channelize_early",
    )(history, rows, jnp.asarray(tables), jnp.asarray(waves), into)


def spread_tables():
    even = np.zeros((INPUTS, INPUTS, 2))
    odd = np.zeros((INPUTS, INPUTS, 2))
    inputs = np.arange(INPUTS).reshape(GROUPS, INPUTS_HERE)[ORDER].reshape(INPUTS)
    even[inputs, np.arange(INPUTS), 0] = 1.0
    odd[inputs, np.arange(INPUTS), 1] = 1.0
    even = even.reshape(INPUTS, 2 * INPUTS)
    odd = odd.reshape(INPUTS, 2 * INPUTS)
    upper = np.concatenate([even, -odd], axis=0)
    lower = np.concatenate([odd, even], axis=0)
    return upper.astype(jnp.bfloat16), lower.astype(jnp.bfloat16)


def weights_kernel(packed_ref, upper, lower, out, ordered):
    for p, device in enumerate(ORDER):
        ordered[pl.ds(BEAMS_HERE * p, BEAMS_HERE), :] = packed_ref[
            pl.ds(BEAMS_HERE * device, BEAMS_HERE), :
        ]
    packed = ordered[...]
    parts = jnp.concatenate(
        [
            ((packed >> 6) - 32).astype(jnp.float32).astype(jnp.bfloat16),
            ((packed & 63) - 32).astype(jnp.float32).astype(jnp.bfloat16),
        ],
        axis=1,
    )
    out[:BEAMS] = jnp.dot(parts, upper[...], preferred_element_type=jnp.float32).astype(
        jnp.bfloat16
    )
    out[BEAMS:] = jnp.dot(parts, lower[...], preferred_element_type=jnp.float32).astype(
        jnp.bfloat16
    )


def stacked_weights(packed):
    upper, lower = spread_tables()
    return pl.pallas_call(
        weights_kernel,
        out_shape=jax.ShapeDtypeStruct((2 * BEAMS, 2 * INPUTS), jnp.bfloat16),
        in_specs=[pl.BlockSpec(memory_space=pltpu.VMEM)] * 3,
        out_specs=pl.BlockSpec(memory_space=pltpu.VMEM),
        scratch_shapes=[pltpu.VMEM((BEAMS, INPUTS), jnp.int32)],
        compiler_params=pltpu.CompilerParams(vmem_limit_bytes=BEAM_VMEM_BYTES),
        cost_estimate=pl.CostEstimate(
            flops=2 * 2 * BEAMS * 512 * 512, bytes_accessed=5 * 2**20, transcendentals=0
        ),
        name="stack_weights",
    )(packed, jnp.asarray(upper), jnp.asarray(lower))


BEAM_BLOCK = 256
CODED_ROWS = 16
SMALLEST_POWER = 2.0**-120


def beams_kernel(weights_ref, spectra_ref, out, total, averaged, coded):
    pairs = range(spectra_ref.shape[1])
    blocks = range(0, BEAMS, BEAM_BLOCK)

    def paired(pair):
        spectra = spectra_ref[:, pair].astype(jnp.float32)
        return jnp.concatenate(
            [
                spectra[:, half * 8 : half * 8 + 8].reshape(2 * INPUTS, SECTION).astype(jnp.bfloat16)
                for half in range(2)
            ],
            axis=1,
        )

    def formed(at, values):
        return jnp.dot(
            weights_ref[at : at + BEAM_BLOCK], values, preferred_element_type=jnp.float32
        )

    values = {}
    for block, at in enumerate(blocks):
        for pair in pairs:
            if block == 0:
                values[pair] = paired(pair)
            real_part = formed(at, values[pair])
            imag_part = formed(BEAMS + at, values[pair])
            powers = real_part * real_part + imag_part * imag_part
            total[at : at + BEAM_BLOCK] = (
                powers if pair == 0 else total[at : at + BEAM_BLOCK] + powers
            )
    scale = 1.0 / (24.0 * math.sqrt(INPUTS)) ** 2 / AVERAGE
    lane = lax.broadcasted_iota(jnp.int32, (BEAMS, SECTION), 1)
    sums = []
    for half in range(2):
        part = total[:, half * SECTION : (half + 1) * SECTION]
        sums.append((part + pltpu.roll(part, OUTER, 1)) * scale)
    averaged[...] = jnp.where(lane < OUTER, sums[0], sums[1])
    lane = lax.broadcasted_iota(jnp.int32, (GROUPS, SECTION), 1)
    exponents = jnp.zeros((GROUPS, SECTION), jnp.float32)
    coded[...] = jnp.zeros_like(coded)
    for beam in range(BEAMS_HERE):
        power = averaged[pl.ds(beam, GROUPS, stride=BEAMS_HERE), :]
        top = jnp.maximum(jnp.max(power, axis=1, keepdims=True), SMALLEST_POWER)
        exponent = jnp.floor(jnp.log2(top)) + 1.0
        steps = jnp.floor(power * jnp.exp2(-exponent) * 32768.0 + 0.5)
        coded[pl.ds(beam, GROUPS, stride=CODED_ROWS), :] = jnp.minimum(steps, 32767.0)
        exponents = jnp.where(lane == beam, exponent, exponents)
    coded[pl.ds(BEAMS_HERE, GROUPS, stride=CODED_ROWS), :] = exponents
    out[...] = coded[...].astype(jnp.int32).astype(jnp.int16).reshape(out.shape)


def beams(weights, spectra):
    pairs = spectra.shape[1]
    return pl.pallas_call(
        beams_kernel,
        in_specs=[pl.BlockSpec(memory_space=pltpu.VMEM)] * 2,
        out_specs=pl.BlockSpec(memory_space=pltpu.VMEM),
        out_shape=jax.ShapeDtypeStruct((GROUPS, CODED_ROWS, SECTION), jnp.int16),
        scratch_shapes=[
            pltpu.VMEM((BEAMS, 2 * SECTION), jnp.float32),
            pltpu.VMEM((BEAMS, SECTION), jnp.float32),
            pltpu.VMEM((GROUPS * CODED_ROWS, SECTION), jnp.float32),
        ],
        compiler_params=pltpu.CompilerParams(vmem_limit_bytes=BEAM_VMEM_BYTES),
        cost_estimate=pl.CostEstimate(
            flops=pairs * 2 * 1536 * 512 * 256,
            bytes_accessed=1536 * 512 * 2 + pairs * 262144 + 768 * 128 * 4,
            transcendentals=0,
        ),
        name="beams",
    )(weights, spectra)


def decode_kernel(coded_ref, out, values):
    values[...] = coded_ref[...].astype(jnp.int32).astype(jnp.float32).reshape(values.shape)
    exponents = values[pl.ds(BEAMS_HERE, GROUPS, stride=CODED_ROWS), :]
    for beam in range(BEAMS_HERE):
        scale = jnp.exp2(exponents[:, beam : beam + 1]) * 2.0**-15
        rows = pl.ds(beam, GROUPS, stride=CODED_ROWS)
        values[rows, :] = values[rows, :] * scale
    for p, device in enumerate(ORDER):
        out[pl.ds(device, BEAMS_HERE, stride=GROUPS), :] = values[
            pl.ds(CODED_ROWS * p, BEAMS_HERE), :
        ]


def decode(coded):
    return pl.pallas_call(
        decode_kernel,
        in_specs=[pl.BlockSpec(memory_space=pltpu.VMEM)],
        out_specs=pl.BlockSpec(memory_space=pltpu.VMEM),
        out_shape=jax.ShapeDtypeStruct((BEAMS_HERE * GROUPS, SECTION), jnp.float32),
        scratch_shapes=[pltpu.VMEM((GROUPS * CODED_ROWS, SECTION), jnp.float32)],
        compiler_params=pltpu.CompilerParams(vmem_limit_bytes=BEAM_VMEM_BYTES),
        name="decode",
    )(coded)


def per_device(voltages, beam_weights):
    inputs_here, own_len = voltages.shape
    pairs = own_len // CHANNELS // 2
    rows = jnp.transpose(voltages.reshape(inputs_here, own_len // SECTION, SECTION), (1, 0, 2))
    rows = rows.reshape(own_len // SECTION * inputs_here, SECTION)
    rim = (TAPS - 1) * FRAME_ROWS
    devices = lax.axis_size("tm")
    history = lax.ppermute(
        rows[rows.shape[0] - rim :] - ZERO_SAMPLE,
        "tm",
        [(i, i + 1) for i in range(devices - 1)],
    )
    tables, waves = channelizer_tables()
    spectra, head = channelize_late(rows, tables, waves, pairs)
    spectra, packed_weights = lax.optimization_barrier((spectra, beam_weights[0]))
    weights = stacked_weights(packed_weights)
    spectra = channelize_early(history, head, tables, waves, spectra)
    spectra, weights = lax.optimization_barrier((spectra, weights))
    turned = lax.all_to_all(spectra, "chan", 0, 0, axis_index_groups=[ORDER], tiled=True)
    coded = beams(weights, turned)
    received = lax.all_to_all(coded, "chan", 0, 0, axis_index_groups=[ORDER], tiled=True)
    return decode(received).reshape(1, BEAMS_HERE, CHANNELS)


def solution(mesh):
    return jax.shard_map(
        per_device,
        mesh=mesh,
        in_specs=(P("chan", "tm"), P("chan", None, None)),
        out_specs=P("tm", "chan", None),
        check_vma=False,
    )
```
